256 devices in a mesh: tile: 4 (over x), morton: 64 (over z, y, core).
Axes of the slice: x: 4, y: 4, z: 8, core: 2. Of those that a mesh axis runs over, the one named last changes fastest.
Arguments:
- features: bfloat16 [4, 262144, 128], P('tile', 'morton'), may hold values from -6 to 6
- neighbours: int32 [4, 262144, 27], P('tile', 'morton'), may hold values from -1 to 2048, as said below
- counts: int32 [4, 32768], P('tile', 'morton'), may hold values from 1 to 8
- owner: int32 [4, 32768], P('tile', 'morton'), may hold values from 0 to 63, as said below
- slot: int32 [4, 32768], P('tile', 'morton'), may hold values from 0 to 511, as said below
- coarse_neighbours: int32 [4, 32768, 27], P('tile', 'morton'), may hold values from -1 to 2047, as said below
- w_first: bfloat16 [3456, 128], replicated, may hold values from -0.109375 to 0.109375
- w_second: bfloat16 [3456, 128], replicated, may hold values from -0.109375 to 0.109375
- w_down: bfloat16 [1024, 256], replicated, may hold values from -0.1875 to 0.1875
- w_coarse: bfloat16 [6912, 256], replicated, may hold values from -0.078125 to 0.078125
- gain_first: float32 [128], replicated, may hold values from 0.1 to 1.9
- gain_second: float32 [128], replicated, may hold values from 0.1 to 1.9
- gain_down: float32 [256], replicated, may hold values from 0.1 to 1.9
- gain_coarse: float32 [256], replicated, may hold values from 0.1 to 1.9
Outputs:
- fine_out: bfloat16 [4, 262144, 128], P('tile', 'morton')
- coarse_out: bfloat16 [4, 32768, 256], P('tile', 'morton')
The draws below stay inside these ranges and needn't reach their ends.
Inputs may be any that keep to these rules, and one draw needn't show every extreme that they name: `neighbours`: entry k of octant r's list is -1 for an absent neighbour, else the neighbour's row minus r plus 1024, and the neighbour lies in the same tile; entry 13 is 1024 (r itself). Block b's first counts octants are real, the rest padding. A block's parent is owned by its own device or by the next or previous Morton index of its tile; a device's blocks with a lower owner form a run at the start of its range, those with a higher owner a run at the end. At most 64 blocks of one device have a given other owner, and in every tile some device hands exactly 64 to a neighbour. Within a tile the pairs (owner, slot) are all distinct, so every parent row is filled exactly once. `coarse_neighbours`: rows are numbered t * 512 + s over the parents of the four tiles with the same Morton range, -1 for an absent neighbour; entry 13 is the parent itself. Most entries lie in the parent's own tile; parents on a tile border have some entries in another tile.
All inputs are finite; a program needn't handle non-finite values.
Results may differ from the reference program's by a relative error of at most 0.009.
Values may be sent and summed in bfloat16 or wider, within the bound.
A program may use at most 128 MiB of HBM per device.

```python
import jax
import jax.numpy as jnp
from jax import lax

C = 128
C2 = 256
BLK_DEV = 512
OCT_DEV = 4096
HALO = 1024
MOST = 64
BLK_TILE = 32768
OCT_TILE = 262144
N_TILE = 4
N_MORTON = 64


def route_plan(key):

    def one_tile(tile_key):
        keys = jax.random.split(tile_key, 2)
        runs = jax.random.randint(keys[0], (N_MORTON - 1,), 1, MOST + 1).astype(jnp.int32)
        peak = jax.random.randint(keys[1], (), 0, N_MORTON - 1)
        runs = jnp.where(jnp.arange(N_MORTON - 1, dtype=jnp.int32) == peak, MOST, runs).astype(jnp.int32)
        zero_one = jnp.zeros((1,), jnp.int32)
        lower = jnp.concatenate([zero_one, runs])[:, None]
        upper = BLK_DEV - jnp.concatenate([runs, zero_one])[:, None]
        device_ids = jnp.arange(N_MORTON, dtype=jnp.int32)[:, None]
        block_ids = jnp.arange(BLK_DEV, dtype=jnp.int32)[None, :]
        owners = jnp.where(block_ids < lower, device_ids - 1, jnp.where(block_ids >= upper, device_ids + 1, device_ids))
        slots = jnp.where(block_ids < lower, BLK_DEV - lower + block_ids, jnp.where(block_ids >= upper, block_ids - upper, block_ids))
        return (owners.reshape(-1).astype(jnp.int32), slots.reshape(-1).astype(jnp.int32))
    return jax.vmap(one_tile)(jax.random.split(key, N_TILE))


def draw_owner(key, part):
    return route_plan(key)[0].astype(jnp.int32)


def draw_slot(key, part):
    return route_plan(key)[1].astype(jnp.int32)


def draw_neighbours(key, part):
    key = jax.random.fold_in(key, 11)
    keys = jax.random.split(key, 3)
    shape = (N_TILE, OCT_TILE, 27)
    kind = jax.random.randint(keys[0], shape, 0, 100)
    near = jax.random.randint(keys[1], shape, -16, 17)
    far = jax.random.randint(keys[2], shape, -HALO, HALO + 1)
    row_ids = jnp.arange(OCT_TILE, dtype=jnp.int32)[None, :, None]
    offset_ids = jnp.arange(27, dtype=jnp.int32)[None, None, :]
    offset = jnp.where(kind < 60, near, far)
    forced = row_ids % 251 == 0
    low_end = forced & (offset_ids == 0)
    high_end = forced & (offset_ids == 26)
    offset = jnp.where(low_end, -HALO, offset)
    offset = jnp.where(high_end, HALO, offset)
    offset = jnp.where(offset_ids == 13, 0, offset)
    target = row_ids + offset
    missing = (kind >= 85) & (offset_ids != 13) & jnp.logical_not(low_end | high_end)
    outside = (target < 0) | (target >= OCT_TILE)
    return jnp.where(missing | outside, -1, offset + HALO).astype(jnp.int32)


def draw_coarse_neighbours(key, part):
    key = jax.random.fold_in(key, 23)
    keys = jax.random.split(key, 4)
    shape = (N_TILE, BLK_TILE, 27)
    kind = jax.random.randint(keys[0], shape, 0, 100)
    offset = jax.random.randint(keys[1], shape, -16, 17)
    border = jax.random.randint(keys[2], (N_TILE, BLK_TILE, 1), 0, 8) == 0
    other_step = jax.random.randint(keys[3], (N_TILE, BLK_TILE, 1), 1, N_TILE)
    offset_ids = jnp.arange(27, dtype=jnp.int32)[None, None, :]
    tile_ids = jnp.arange(N_TILE, dtype=jnp.int32)[:, None, None]
    own_s = (jnp.arange(BLK_TILE, dtype=jnp.int32) % BLK_DEV)[None, :, None]
    row = own_s + offset
    across = border & (offset_ids < 9)
    tile_used = jnp.where(across, (tile_ids + other_step) % N_TILE, tile_ids)
    picked = tile_used * BLK_DEV + row
    absent = (kind < 15) | (row < 0) | (row >= BLK_DEV)
    picked = jnp.where(absent, -1, picked)
    return jnp.where(offset_ids == 13, tile_ids * BLK_DEV + own_s, picked).astype(jnp.int32)


def place_ends(result, key, least, largest):
    extent = result.shape
    place = [jax.random.randint(jax.random.fold_in(key, axis), (), 0, extent[axis]) for axis in range(len(extent))]
    result = result.at[tuple(place)].set(least)
    longest = extent.index(max(extent))
    place[longest] = (place[longest] + 1) % extent[longest]
    return result.at[tuple(place)].set(largest)


def steps_of(stream_key, dims, pieces, smallest, top_value):
    level = 1.0
    for dim, blocks in pieces:
        heights = jax.random.uniform(jax.random.fold_in(jax.random.fold_in(stream_key, 6), dim), (blocks,), jnp.float32, smallest / len(pieces), top_value / len(pieces))
        level = level * jnp.repeat(jnp.exp(heights), dims[dim] // blocks).reshape((-1,) + (1,) * (len(dims) - 1 - dim))
    return level


def gaussian(rng, shape, width, most, cuts=(), kind=jnp.bfloat16):
    drawn = jax.random.normal(rng, shape, jnp.float32) * width
    if len(cuts) > 0:
        drawn = steps_of(rng, shape, cuts, -0.22, 0.18) * drawn
    return jnp.clip(drawn, min=-most, max=most).astype(kind)


def setup_inputs(seed: int = 0) -> dict:
    streams_of = jax.random.split(jax.random.key(seed), 15)
    features = gaussian(streams_of[0], (N_TILE, OCT_TILE, C), 1.0, 6.0, ((0, 4), (1, 64)))
    neighbours = draw_neighbours(jax.random.fold_in(streams_of[14], 71), 0)
    counts = place_ends(jax.random.randint(streams_of[2], (N_TILE, BLK_TILE), 1, 9), jax.random.fold_in(streams_of[2], 1), 1, 8).astype(jnp.int32)
    owner = draw_owner(jax.random.fold_in(streams_of[14], 71), 0)
    slot = draw_slot(jax.random.fold_in(streams_of[14], 71), 0)
    coarse_neighbours = draw_coarse_neighbours(jax.random.fold_in(streams_of[14], 71), 0)
    w_first = gaussian(streams_of[6], (27 * C, C), (27 * C) ** -0.5, 0.109375)
    w_second = gaussian(streams_of[7], (27 * C, C), (27 * C) ** -0.5, 0.109375)
    w_down = gaussian(streams_of[8], (8 * C, C2), (8 * C) ** -0.5, 0.1875)
    w_coarse = gaussian(streams_of[9], (27 * C2, C2), (27 * C2) ** -0.5, 0.078125)
    gain_first = jnp.clip(1.0 + 0.18 * jax.random.normal(streams_of[10], (C,), jnp.float32), 0.1, 1.9)
    gain_second = jnp.clip(1.0 + 0.18 * jax.random.normal(streams_of[11], (C,), jnp.float32), 0.1, 1.9)
    gain_down = jnp.clip(1.0 + 0.18 * jax.random.normal(streams_of[12], (C2,), jnp.float32), 0.1, 1.9)
    gain_coarse = jnp.clip(1.0 + 0.18 * jax.random.normal(streams_of[13], (C2,), jnp.float32), 0.1, 1.9)
    return {"features": features, "neighbours": neighbours, "counts": counts, "owner": owner, "slot": slot, "coarse_neighbours": coarse_neighbours, "w_first": w_first, "w_second": w_second, "w_down": w_down, "w_coarse": w_coarse, "gain_first": gain_first, "gain_second": gain_second, "gain_down": gain_down, "gain_coarse": gain_coarse}


def rms_scale(values, gain):
    return values * lax.rsqrt(lax.optimization_barrier(jnp.mean(values * values, axis=-1, keepdims=True)) + 1e-05) * gain

def conv_tile(field, index_rows, weight):
    padded = jnp.concatenate([field, jnp.zeros((1, field.shape[1]), field.dtype)], axis=0)
    row_ids = jnp.arange(OCT_TILE, dtype=jnp.int32)[:, None]
    target = (row_ids + index_rows - HALO).astype(jnp.int32)
    safe_idx = jnp.where(index_rows < 0, OCT_TILE, target).astype(jnp.int32)
    grouped = safe_idx.reshape(N_MORTON, OCT_DEV, 27)

    def one_block(block_idx):
        taken = jnp.take(padded, block_idx, axis=0).reshape(OCT_DEV, -1)
        return jnp.dot(taken, weight, preferred_element_type=jnp.float32)
    return lax.map(one_block, grouped).reshape(OCT_TILE, weight.shape[1])

def reference(features, neighbours, counts, owner, slot, coarse_neighbours, w_first, w_second, w_down, w_coarse, gain_first, gain_second, gain_down, gain_coarse):
    lane_ids = jnp.arange(8, dtype=jnp.int32)
    valid = (lane_ids[None, None, :] < counts[:, :, None]).astype(jnp.float32).reshape(N_TILE, OCT_TILE, 1)
    field_in = (features.astype(jnp.float32) * valid).astype(jnp.bfloat16)

    def fine_tile(inputs):
        tile_field, tile_idx, tile_valid = inputs
        first_pre = conv_tile(tile_field, tile_idx, w_first)
        first_act = (tile_valid * jax.nn.relu(rms_scale(first_pre, gain_first))).astype(jnp.bfloat16)
        second_pre = conv_tile(first_act, tile_idx, w_second)
        summed = tile_field.astype(jnp.float32) + rms_scale(second_pre, gain_second)
        return (tile_valid * jax.nn.relu(summed)).astype(jnp.bfloat16)
    fine_out = lax.map(fine_tile, (field_in, neighbours, valid))
    children = fine_out.reshape(N_TILE, BLK_TILE, 8 * C)

    def down_tile(child_rows):
        down_pre = jnp.dot(child_rows, w_down, preferred_element_type=jnp.float32)
        return jax.nn.relu(rms_scale(down_pre, gain_down)).astype(jnp.bfloat16)
    parent_rows = lax.map(down_tile, children)
    position = (owner * BLK_DEV + slot).astype(jnp.int32)

    def place_tile(rows_in, where_to):
        return jnp.zeros((BLK_TILE, C2), jnp.bfloat16).at[where_to].set(rows_in)
    parents = jax.vmap(place_tile)(parent_rows, position)
    parents_grid = parents.reshape(N_TILE, N_MORTON, BLK_DEV, C2)
    coarse_grid = coarse_neighbours.reshape(N_TILE, N_MORTON, BLK_DEV, 27)

    def coarse_one(flat_at):
        tile_at = flat_at // N_MORTON
        morton_at = flat_at % N_MORTON
        pooled = lax.dynamic_index_in_dim(parents_grid, morton_at, axis=1, keepdims=False).reshape(N_TILE * BLK_DEV, C2)
        pooled = jnp.concatenate([pooled, jnp.zeros((1, C2), jnp.bfloat16)], axis=0)
        own_rows = parents_grid[tile_at, morton_at]
        index_rows = coarse_grid[tile_at, morton_at]
        safe_idx = jnp.where(index_rows < 0, N_TILE * BLK_DEV, index_rows).astype(jnp.int32)
        taken = jnp.take(pooled, safe_idx, axis=0).reshape(BLK_DEV, -1)
        coarse_pre = jnp.dot(taken, w_coarse, preferred_element_type=jnp.float32)
        return jax.nn.relu(own_rows.astype(jnp.float32) + rms_scale(coarse_pre, gain_coarse)).astype(jnp.bfloat16)
    coarse_out = lax.map(coarse_one, jnp.arange(N_TILE * N_MORTON, dtype=jnp.int32)).reshape(N_TILE, BLK_TILE, C2)
    return (fine_out, coarse_out)
```

```python
import functools

import jax
import jax.numpy as jnp
from jax import lax
from jax.experimental import pallas as pl
from jax.experimental.pallas import tpu as pltpu
from jax.sharding import PartitionSpec as P

K = 27
TILE = 128
GROUPS = TILE // 16
PAD = 8
EPS = 1e-05
VMEM_LIMIT = 58 * 2**20


def shifted(value, axis, steps):
    count = lax.axis_size(axis)
    initial, last = (max(0, -steps), min(count, count - steps))
    return lax.ppermute(value, axis, [(source, source + steps) for source in range(initial, last)])


def sublane_masks():
    sub = lax.broadcasted_iota(jnp.int32, (8, 128), 0)
    return [sub == i for i in range(8)]


def gather_group(idx_ref, tables, dst_ref, tile, sub, masks):
    halves = len(tables)
    width = 128 * halves
    for k in range(K):
        refs = idx_ref.at[pl.ds(tile * (K * TILE) + k * TILE + sub * 16, 16)]
        parts = [[], []]
        rows = [[None] * 8 for _ in range(2)]
        for h in range(2):
            for i in range(8):
                rows[h][i] = refs[h * 8 + i]
        for n, (table, base) in enumerate(tables):
            both = []
            for h in range(2):
                acc = None
                for i in range(8):
                    v = table[pl.ds(rows[h][i] + (base + PAD - i), 8), :]
                    acc = v if acc is None else jnp.where(masks[i], v, acc)
                both.append(acc)
            col = (k % 4) * width + n * 128
            dst_ref[k // 4, pl.ds(pl.multiple_of(sub * 16, 16), 16), col : col + 128] = jnp.concatenate(
                both, 0
            ).astype(jnp.bfloat16)


def run_tiles(idx_ref, tables, w_ref, ga, gb, acc_ref, pairs, first_tile, masks, epilogue):
    def half(tile, dst, src):
        def body(j, _):
            acc_ref[...] += jnp.dot(src[j], w_ref[j], preferred_element_type=jnp.float32)
            gather_group(idx_ref, tables, dst, tile, j, masks)
            return 0

        lax.fori_loop(0, GROUPS, body, 0)
        epilogue(jnp.maximum(first_tile + tile - 1, 0))
        acc_ref[...] = jnp.zeros_like(acc_ref)

    def pair(p, _):
        half(2 * p, ga, gb)
        half(2 * p + 1, gb, ga)
        return 0

    lax.fori_loop(0, pairs, pair, 0)


def drain(w_ref, gb, acc_ref):
    def body(j, _):
        acc_ref[...] += jnp.dot(gb[j], w_ref[j], preferred_element_type=jnp.float32)
        return 0

    lax.fori_loop(0, GROUPS, body, 0)


def pad_weight(w_in, w_ref, width):
    for c in range(7):
        rows = 4 * width if c < 6 else 3 * width
        w_ref[c, :rows, :] = w_in[c * 4 * width : c * 4 * width + rows, :]
    w_ref[6, 3 * width :, :] = jnp.zeros((width, w_ref.shape[2]), w_ref.dtype)
    w_ref[7, :, :] = jnp.zeros((4 * width, w_ref.shape[2]), w_ref.dtype)


def zero_buffers(ga, gb, acc_ref, width):
    for g in (ga, gb):
        g[6, :, 3 * width :] = jnp.zeros((TILE, width), g.dtype)
        g[7, :, :] = jnp.zeros((TILE, 4 * width), g.dtype)
    acc_ref[...] = jnp.zeros_like(acc_ref)


def normed(h, gain):
    return h * lax.rsqrt(jnp.mean(h * h, axis=-1, keepdims=True) + EPS) * gain


def conv_kernel(
    second,
    idx_ref,
    counts_ref,
    lo_ref,
    mid_ref,
    hi_ref,
    w_in,
    gain_ref,
    *rest,
):
    if second:
        x_ref, wd_ref, gain_down_ref, out_ref, down_ref, table, w_ref, ga, gb, acc_ref, fine_ref = rest
    else:
        out_ref, table, w_ref, ga, gb, acc_ref = rest
    step = pl.program_id(0)
    masks = sublane_masks()
    sub16 = lax.broadcasted_iota(jnp.int32, (8, 128), 0)

    @pl.when(step == 0)
    def _():
        table[:PAD, :] = jnp.zeros((PAD, 128), jnp.float32)
        table[pl.ds(PAD, 1024), :] = lo_ref[...].astype(jnp.float32)
        table[pl.ds(PAD + 1024, 4096), :] = mid_ref[...].astype(jnp.float32)
        table[pl.ds(PAD + 5120, 1024), :] = hi_ref[...].astype(jnp.float32)
        pad_weight(w_in, w_ref, 128)
        zero_buffers(ga, gb, acc_ref, 128)

    def epilogue(tile):
        gain = gain_ref[...]
        for i in range(GROUPS):
            h = normed(acc_ref[i * 16 : (i + 1) * 16, :], gain)
            row = pl.multiple_of(tile * TILE + i * 16, 16)
            if second:
                h = x_ref[pl.ds(row, 16), :].astype(jnp.float32) + h
            valid = jnp.concatenate(
                [sub16 < counts_ref[tile * GROUPS * 2 + 2 * i], sub16 < counts_ref[tile * GROUPS * 2 + 2 * i + 1]], 0
            )
            value = jnp.where(valid, jnp.maximum(h, 0.0), 0.0).astype(jnp.bfloat16)
            out_ref[pl.ds(row, 16), :] = value
            if second:
                fine_ref[pl.ds(row, 16), :] = value.astype(jnp.float32)

    run_tiles(idx_ref, ((table, 0),), w_ref, ga, gb, acc_ref, 4, step * 8, masks, epilogue)

    @pl.when(step == 3)
    def _():
        drain(w_ref, gb, acc_ref)
        epilogue(31)
        if second:

            def down(c, _):
                total = jnp.zeros((64, 256), jnp.float32)
                for j in range(8):
                    child = fine_ref[pl.ds(c * 512 + j, 64, stride=8), :].astype(jnp.bfloat16)
                    total += jnp.dot(child, wd_ref[j * 128 : (j + 1) * 128, :], preferred_element_type=jnp.float32)
                value = jnp.maximum(normed(total, gain_down_ref[...]), 0.0)
                down_ref[pl.ds(pl.multiple_of(c * 64, 64), 64), :] = value.astype(jnp.bfloat16)
                return 0

            lax.fori_loop(0, 8, down, 0)


def whole(shape):
    return pl.BlockSpec(shape, lambda i: (0,) * len(shape))


def conv(second, idx, counts, lo, mid, hi, w, gain, *more):
    specs = [
        pl.BlockSpec((8 * K * TILE,), lambda i: (i,), memory_space=pltpu.SMEM),
        pl.BlockSpec(memory_space=pltpu.SMEM),
    ] + [whole(a.shape) for a in (lo, mid, hi, w, gain) + more]
    out_shape = [jax.ShapeDtypeStruct((4096, 128), jnp.bfloat16)]
    scratch = [
        pltpu.VMEM((PAD + 6144 + 8, 128), jnp.float32),
        pltpu.VMEM((8, 512, 128), jnp.bfloat16),
        pltpu.VMEM((8, TILE, 512), jnp.bfloat16),
        pltpu.VMEM((8, TILE, 512), jnp.bfloat16),
        pltpu.VMEM((TILE, 128), jnp.float32),
    ]
    if second:
        out_shape.append(jax.ShapeDtypeStruct((512, 256), jnp.bfloat16))
        scratch.append(pltpu.VMEM((4096, 128), jnp.float32))
    return pl.pallas_call(
        functools.partial(conv_kernel, second),
        grid=(4,),
        in_specs=specs,
        out_specs=[whole(s.shape) for s in out_shape],
        out_shape=out_shape,
        scratch_shapes=scratch,
        name="conv_second" if second else "conv_first",
        compiler_params=pltpu.CompilerParams(vmem_limit_bytes=VMEM_LIMIT),
    )(idx, counts, lo, mid, hi, w, gain, *more)


def place_kernel(pos_ref, own_ref, below_ref, above_ref, out_ref, src, dst):
    src[:512, :] = own_ref[:, :128].astype(jnp.float32)
    src[512:576, :] = below_ref[:, :128].astype(jnp.float32)
    src[576:640, :] = above_ref[:, :128].astype(jnp.float32)
    src[640:1152, :] = own_ref[:, 128:].astype(jnp.float32)
    src[1152:1216, :] = below_ref[:, 128:].astype(jnp.float32)
    src[1216:1280, :] = above_ref[:, 128:].astype(jnp.float32)

    def body(g, _):
        for i in range(16):
            at = pos_ref[g * 16 + i]
            dst[pl.ds(at, 1), :] = src[pl.ds(g * 16 + i, 1), :]
            dst[pl.ds(at + 520, 1), :] = src[pl.ds(g * 16 + i + 640, 1), :]
        return 0

    lax.fori_loop(0, 40, body, 0)
    out_ref[:, :128] = dst[:512, :].astype(jnp.bfloat16)
    out_ref[:, 128:] = dst[520:1032, :].astype(jnp.bfloat16)


def place(pos, own, below, above):
    return pl.pallas_call(
        place_kernel,
        in_specs=[pl.BlockSpec(memory_space=pltpu.SMEM)] + [pl.BlockSpec(memory_space=pltpu.VMEM)] * 3,
        out_specs=pl.BlockSpec(memory_space=pltpu.VMEM),
        out_shape=jax.ShapeDtypeStruct((512, 256), jnp.bfloat16),
        scratch_shapes=[pltpu.VMEM((1280, 128), jnp.float32), pltpu.VMEM((1040, 128), jnp.float32)],
        name="place",
    )(pos, own, below, above)


HALF = 2048 + 16


def coarse_kernel(idx_ref, pool_ref, own_ref, w_in, gain_ref, out_ref, table, w_ref, ga, gb, acc_ref):
    masks = sublane_masks()
    table[:PAD, :] = jnp.zeros((PAD, 128), jnp.float32)
    table[HALF : HALF + PAD, :] = jnp.zeros((PAD, 128), jnp.float32)
    table[pl.ds(PAD, 2048), :] = pool_ref[:, :128].astype(jnp.float32)
    table[pl.ds(HALF + PAD, 2048), :] = pool_ref[:, 128:].astype(jnp.float32)
    pad_weight(w_in, w_ref, 256)
    zero_buffers(ga, gb, acc_ref, 256)

    def epilogue(tile):
        for i in range(GROUPS):
            h = normed(acc_ref[i * 16 : (i + 1) * 16, :], gain_ref[...])
            row = pl.multiple_of(tile * TILE + i * 16, 16)
            h = own_ref[pl.ds(row, 16), :].astype(jnp.float32) + h
            out_ref[pl.ds(row, 16), :] = jnp.maximum(h, 0.0).astype(jnp.bfloat16)

    run_tiles(idx_ref, ((table, 0), (table, HALF)), w_ref, ga, gb, acc_ref, 2, 0, masks, epilogue)
    drain(w_ref, gb, acc_ref)
    epilogue(3)


def coarse(idx, pool, own, w, gain):
    return pl.pallas_call(
        coarse_kernel,
        in_specs=[pl.BlockSpec(memory_space=pltpu.SMEM)] + [pl.BlockSpec(memory_space=pltpu.VMEM)] * 4,
        out_specs=pl.BlockSpec(memory_space=pltpu.VMEM),
        out_shape=jax.ShapeDtypeStruct((512, 256), jnp.bfloat16),
        scratch_shapes=[
            pltpu.VMEM((2 * HALF, 128), jnp.float32),
            pltpu.VMEM((8, 1024, 256), jnp.bfloat16),
            pltpu.VMEM((8, TILE, 1024), jnp.bfloat16),
            pltpu.VMEM((8, TILE, 1024), jnp.bfloat16),
            pltpu.VMEM((TILE, 256), jnp.float32),
        ],
        name="coarse",
        compiler_params=pltpu.CompilerParams(vmem_limit_bytes=VMEM_LIMIT),
    )(idx, pool, own, w, gain)


def by_tiles(index):
    rows = index.shape[1]
    return index.reshape(K, rows // TILE, TILE).transpose(1, 0, 2).reshape(-1)


def shards(
    features,
    neighbours,
    counts,
    owner,
    slot,
    coarse_neighbours,
    w_first,
    w_second,
    w_down,
    w_coarse,
    gain_first,
    gain_second,
    gain_down,
    gain_coarse,
):
    lane_ids = jnp.arange(8, dtype=jnp.int32)
    valid = lane_ids[None, :] < counts[0][:, None]
    field = jnp.where(valid[:, :, None], features[0].reshape(512, 8, 128), 0).astype(jnp.bfloat16).reshape(4096, 128)
    by_offset = neighbours[0].T
    local = by_offset + jnp.arange(4096, dtype=jnp.int32)[None, :]
    idx = by_tiles(jnp.where(by_offset < 0, -1, local))
    coarse_idx = by_tiles(coarse_neighbours[0].T)

    me = lax.axis_index("morton")
    destination, plus = owner[0], slot[0] + 1
    own_at = jnp.where(destination == me, plus, 0)
    below_at = shifted(jnp.where(destination == me + 1, plus, 0)[448:], "morton", 1)
    above_at = shifted(jnp.where(destination == me - 1, plus, 0)[:64], "morton", -1)
    at = jnp.concatenate([own_at, below_at, above_at])
    at = jnp.where(at > 0, at - 1, 512)

    def halo(v):
        return shifted(v[3072:], "morton", 1), shifted(v[:1024], "morton", -1)

    lo, hi = halo(field)
    (act,) = conv(False, idx, counts[0], lo, field, hi, w_first, gain_first[None])
    lo, hi = halo(act)
    fine, rows = conv(
        True, idx, counts[0], lo, act, hi, w_second, gain_second[None], field, w_down, gain_down[None]
    )
    below, above = shifted(rows[448:], "morton", 1), shifted(rows[:64], "morton", -1)
    parents = place(at, rows, below, above)
    pool = lax.all_gather(parents, "tile", axis=0, tiled=True)
    out = coarse(coarse_idx, pool, parents, w_coarse, gain_coarse[None])
    return fine[None], out[None]


def solution(mesh):
    split = P("tile", "morton", None)
    flat = P("tile", "morton")
    in_specs = (split, split, flat, flat, flat, split) + (P(),) * 8
    return jax.shard_map(shards, mesh=mesh, in_specs=in_specs, out_specs=(split, split), check_vma=False)
```

```python
import functools

import jax
import jax.numpy as jnp
from jax import lax
from jax.experimental import pallas as pl
from jax.experimental.pallas import tpu as pltpu
from jax.sharding import PartitionSpec as P

K = 27
TILE = 128
GROUPS = TILE // 16
PAD = 8
EPS = 1e-05
VMEM_LIMIT = 58 * 2**20


def shifted(value, axis, steps):
    count = lax.axis_size(axis)
    initial, last = (max(0, -steps), min(count, count - steps))
    return lax.ppermute(value, axis, [(source, source + steps) for source in range(initial, last)])


def sublane_masks():
    sub = lax.broadcasted_iota(jnp.int32, (8, 128), 0)
    return [sub == i for i in range(8)]


def gather_rows(idx_ref, tables, dst_ref, tiles, masks):
    width = 128 * len(tables)

    def body(g, _):
        base_ref = idx_ref.at[pl.ds((g // GROUPS) * (K * TILE) + (g % GROUPS) * 16, (K - 1) * TILE + 16)]
        for k in range(K):
            both = [[] for _ in tables]
            for h in range(2):
                at = base_ref.at[pl.ds(k * TILE + h * 8, 8)]
                acc = [None for _ in tables]
                for i in range(8):
                    row = at[i]
                    for n, (table, base) in enumerate(tables):
                        v = table[pl.ds(row + (base + PAD - i), 8), :]
                        acc[n] = v if i == 0 else jnp.where(masks[i], v, acc[n])
                for n in range(len(tables)):
                    both[n].append(acc[n])
            for n in range(len(tables)):
                col = k * width + n * 128
                dst_ref[pl.ds(pl.multiple_of(g * 16, 16), 16), col : col + 128] = jnp.concatenate(
                    both[n], 0
                ).astype(jnp.bfloat16)
        return 0

    lax.fori_loop(0, tiles * GROUPS, body, 0)


def normed(h, gain):
    return h * lax.rsqrt(jnp.mean(h * h, axis=-1, keepdims=True) + EPS) * gain


def conv_kernel(
    second,
    idx_ref,
    counts_ref,
    lo_ref,
    mid_ref,
    hi_ref,
    w_in,
    gain_ref,
    *rest,
):
    if second:
        x_ref, wd_ref, gain_down_ref, out_ref, down_ref, table, gathered, acc_ref, fine_ref = rest
    else:
        out_ref, table, gathered, acc_ref = rest
    step = pl.program_id(0)
    masks = sublane_masks()
    sub16 = lax.broadcasted_iota(jnp.int32, (8, 128), 0)

    @pl.when(step == 0)
    def _():
        table[:PAD, :] = jnp.zeros((PAD, 128), jnp.float32)
        table[pl.ds(PAD, 1024), :] = lo_ref[...].astype(jnp.float32)
        table[pl.ds(PAD + 1024, 4096), :] = mid_ref[...].astype(jnp.float32)
        table[pl.ds(PAD + 5120, 1024), :] = hi_ref[...].astype(jnp.float32)

    gather_rows(idx_ref, ((table, 0),), gathered, 8, masks)
    acc_ref[...] = jnp.dot(gathered[...], w_in[...], preferred_element_type=jnp.float32)

    def epilogue(tile, _):
        gain = gain_ref[...]
        for i in range(GROUPS):
            h = normed(acc_ref[pl.ds(pl.multiple_of(tile * TILE + i * 16, 16), 16), :], gain)
            row = pl.multiple_of(step * 1024 + tile * TILE + i * 16, 16)
            if second:
                h = x_ref[pl.ds(row, 16), :].astype(jnp.float32) + h
            block = step * 128 + tile * GROUPS * 2 + 2 * i
            valid = jnp.concatenate([sub16 < counts_ref[block], sub16 < counts_ref[block + 1]], 0)
            value = jnp.where(valid, jnp.maximum(h, 0.0), 0.0).astype(jnp.bfloat16)
            out_ref[pl.ds(row, 16), :] = value
            if second:
                fine_ref[pl.ds(row, 16), :] = value.astype(jnp.float32)
        return 0

    lax.fori_loop(0, 8, epilogue, 0)

    if second:

        @pl.when(step == 3)
        def _():

            def down(c, _):
                total = jnp.zeros((64, 256), jnp.float32)
                for j in range(8):
                    child = fine_ref[pl.ds(c * 512 + j, 64, stride=8), :].astype(jnp.bfloat16)
                    total += jnp.dot(child, wd_ref[j * 128 : (j + 1) * 128, :], preferred_element_type=jnp.float32)
                value = jnp.maximum(normed(total, gain_down_ref[...]), 0.0)
                down_ref[pl.ds(pl.multiple_of(c * 64, 64), 64), :] = value.astype(jnp.bfloat16)
                return 0

            lax.fori_loop(0, 8, down, 0)


def whole(shape):
    return pl.BlockSpec(shape, lambda i: (0,) * len(shape))


def conv(second, idx, counts, lo, mid, hi, w, gain, *more):
    specs = [
        pl.BlockSpec((8 * K * TILE,), lambda i: (i,), memory_space=pltpu.SMEM),
        pl.BlockSpec(memory_space=pltpu.SMEM),
    ] + [whole(a.shape) for a in (lo, mid, hi, w, gain) + more]
    out_shape = [jax.ShapeDtypeStruct((4096, 128), jnp.bfloat16)]
    scratch = [
        pltpu.VMEM((PAD + 6144 + 8, 128), jnp.float32),
        pltpu.VMEM((1024, K * 128), jnp.bfloat16),
        pltpu.VMEM((1024, 128), jnp.float32),
    ]
    if second:
        out_shape.append(jax.ShapeDtypeStruct((512, 256), jnp.bfloat16))
        scratch.append(pltpu.VMEM((4096, 128), jnp.float32))
    return pl.pallas_call(
        functools.partial(conv_kernel, second),
        grid=(4,),
        in_specs=specs,
        out_specs=[whole(s.shape) for s in out_shape],
        out_shape=out_shape,
        scratch_shapes=scratch,
        name="conv_second" if second else "conv_first",
        compiler_params=pltpu.CompilerParams(vmem_limit_bytes=VMEM_LIMIT),
    )(idx, counts, lo, mid, hi, w, gain, *more)


HALF = 2048 + 16
NOWHERE = PAD + 2048
REACH = 640


def exchange_kernel(rows_ref, codes_ref, pool_ref, places_ref, send_sem, recv_sem, local_sem):
    tile, me = lax.axis_index("tile"), lax.axis_index("morton")
    tiles, ranges = lax.axis_size("tile"), lax.axis_size("morton")
    above, below = lax.rem(me + 1, ranges), lax.rem(me + ranges - 1, ranges)
    peers = [lax.rem(tile + d, tiles) for d in range(tiles)]

    barrier = pltpu.get_barrier_semaphore()
    partners = [(peers[d], me) for d in range(1, tiles)] + [(peers[d], m) for m in (above, below) for d in range(tiles)]
    for partner in partners:
        pl.semaphore_signal(barrier, inc=1, device_id=partner, device_id_type=pl.DeviceIdType.MESH)
    pl.semaphore_wait(barrier, len(partners))

    copies = []

    def send(src, dst, partner):
        n = len(copies)
        copy = pltpu.make_async_remote_copy(
            src_ref=src,
            dst_ref=dst,
            send_sem=send_sem.at[n],
            recv_sem=recv_sem.at[n],
            device_id=partner,
            device_id_type=pl.DeviceIdType.MESH,
        )
        copy.start()
        copies.append(copy)

    for d in (2, 1, 3):
        send(rows_ref, pool_ref.at[tile, pl.ds(0, 512)], (peers[d], me))
        send(codes_ref.at[0], places_ref.at[0, tile], (peers[d], me))
    for d in range(tiles):
        send(rows_ref.at[pl.ds(448, 64)], pool_ref.at[tile, pl.ds(512, 64)], (peers[d], above))
        send(codes_ref.at[1], places_ref.at[1, tile], (peers[d], above))
        send(rows_ref.at[pl.ds(0, 64)], pool_ref.at[tile, pl.ds(576, 64)], (peers[d], below))
        send(codes_ref.at[1], places_ref.at[2, tile], (peers[d], below))
    own = [
        pltpu.make_async_copy(rows_ref, pool_ref.at[tile, pl.ds(0, 512)], local_sem.at[0]),
        pltpu.make_async_copy(codes_ref.at[0], places_ref.at[0, tile], local_sem.at[1]),
    ]
    for copy in own:
        copy.start()
    for copy in own + copies:
        copy.wait()


def exchange(rows, codes):
    return pl.pallas_call(
        exchange_kernel,
        in_specs=[pl.BlockSpec(memory_space=pl.ANY)] * 2,
        out_specs=[pl.BlockSpec(memory_space=pl.ANY)] * 2,
        out_shape=[
            jax.ShapeDtypeStruct((4, REACH, 256), jnp.bfloat16),
            jax.ShapeDtypeStruct((3, 4, 8, 128), jnp.int32),
        ],
        scratch_shapes=[
            pltpu.SemaphoreType.DMA((22,)),
            pltpu.SemaphoreType.DMA((22,)),
            pltpu.SemaphoreType.DMA((2,)),
        ],
        name="exchange",
        compiler_params=pltpu.CompilerParams(collective_id=0, has_side_effects=True),
    )(rows, codes)


def coarse_kernel(idx_ref, places_ref, pool_ref, w_in, gain_ref, out_ref, table, source, gathered, acc_ref):
    masks = sublane_masks()
    table[:PAD, :] = jnp.zeros((PAD, 128), jnp.float32)
    table[HALF : HALF + PAD, :] = jnp.zeros((PAD, 128), jnp.float32)

    def tile_rows(t, _):
        source[:REACH, :] = pool_ref[t, :, :128].astype(jnp.float32)
        source[REACH:, :] = pool_ref[t, :, 128:].astype(jnp.float32)

        def put(kind, line, col, row):
            for i in range(16):
                at = places_ref[kind, t, line, col + i]
                table[pl.ds(at, 1), :] = source[pl.ds(row + i, 1), :]
                table[pl.ds(at + HALF, 1), :] = source[pl.ds(row + i + REACH, 1), :]

        def own(g, _):
            put(0, g // 8, (g % 8) * 16, pl.multiple_of(g * 16, 16))
            return 0

        lax.fori_loop(0, 32, own, 0)
        for g in range(4):
            put(1, 0, g * 16, 512 + g * 16)
            put(2, 0, 64 + g * 16, 576 + g * 16)
        return 0

    lax.fori_loop(0, 4, tile_rows, 0)
    gather_rows(idx_ref, ((table, 0), (table, HALF)), gathered, 4, masks)
    acc_ref[...] = jnp.dot(gathered[...], w_in[...], preferred_element_type=jnp.float32)
    first = PAD + 512 * lax.axis_index("tile")

    def epilogue(tile, _):
        for i in range(GROUPS):
            row = pl.multiple_of(tile * TILE + i * 16, 16)
            h = normed(acc_ref[pl.ds(row, 16), :], gain_ref[...])
            at = pl.multiple_of(first + row, 8)
            own = jnp.concatenate([table[pl.ds(at, 16), :], table[pl.ds(at + HALF, 16), :]], 1)
            out_ref[pl.ds(row, 16), :] = jnp.maximum(own + h, 0.0).astype(jnp.bfloat16)
        return 0

    lax.fori_loop(0, 4, epilogue, 0)


def coarse(idx, places, pool, w, gain):
    return pl.pallas_call(
        coarse_kernel,
        in_specs=[pl.BlockSpec(memory_space=pltpu.SMEM)] * 2 + [pl.BlockSpec(memory_space=pltpu.VMEM)] * 3,
        out_specs=pl.BlockSpec(memory_space=pltpu.VMEM),
        out_shape=jax.ShapeDtypeStruct((512, 256), jnp.bfloat16),
        scratch_shapes=[
            pltpu.VMEM((2 * HALF, 128), jnp.float32),
            pltpu.VMEM((2 * REACH, 128), jnp.float32),
            pltpu.VMEM((512, K * 256), jnp.bfloat16),
            pltpu.VMEM((512, 256), jnp.float32),
        ],
        name="coarse",
        compiler_params=pltpu.CompilerParams(vmem_limit_bytes=VMEM_LIMIT),
    )(idx, places, pool, w, gain)


def by_tiles(index):
    rows = index.shape[1]
    return index.reshape(K, rows // TILE, TILE).transpose(1, 0, 2).reshape(-1)


def shards(
    features,
    neighbours,
    counts,
    owner,
    slot,
    coarse_neighbours,
    w_first,
    w_second,
    w_down,
    w_coarse,
    gain_first,
    gain_second,
    gain_down,
    gain_coarse,
):
    lane_ids = jnp.arange(8, dtype=jnp.int32)
    valid = lane_ids[None, :] < counts[0][:, None]
    field = jnp.where(valid[:, :, None], features[0].reshape(512, 8, 128), 0).astype(jnp.bfloat16).reshape(4096, 128)
    by_offset = neighbours[0].T
    local = by_offset + jnp.arange(4096, dtype=jnp.int32)[None, :]
    idx = by_tiles(jnp.where(by_offset < 0, -1, local))
    coarse_idx = by_tiles(coarse_neighbours[0].T)

    me = lax.axis_index("morton")
    destination = owner[0]
    at = PAD + 512 * lax.axis_index("tile") + slot[0]

    def handed(to):
        return jnp.where(destination == to, at, NOWHERE)

    edges = jnp.concatenate([handed(me + 1)[448:], handed(me - 1)[:64]])
    codes = jnp.stack([handed(me).reshape(4, 128), jnp.broadcast_to(edges[None], (4, 128))])
    codes = jnp.concatenate([codes, codes], axis=1)

    def halo(v):
        return shifted(v[3072:], "morton", 1), shifted(v[:1024], "morton", -1)

    lo, hi = halo(field)
    (act,) = conv(False, idx, counts[0], lo, field, hi, w_first, gain_first[None])
    lo, hi = halo(act)
    fine, rows = conv(
        True, idx, counts[0], lo, act, hi, w_second, gain_second[None], field, w_down, gain_down[None]
    )
    pool, places = exchange(rows, codes)
    out = coarse(coarse_idx, places, pool, w_coarse, gain_coarse[None])
    return fine[None], out[None]


def solution(mesh):
    split = P("tile", "morton", None)
    flat = P("tile", "morton")
    in_specs = (split, split, flat, flat, flat, split) + (P(),) * 8
    return jax.shard_map(shards, mesh=mesh, in_specs=in_specs, out_specs=(split, split), check_vma=False)
```

```python
import functools

import jax
import jax.numpy as jnp
from jax import lax
from jax.experimental import pallas as pl
from jax.experimental.pallas import tpu as pltpu
from jax.sharding import PartitionSpec as P

K = 27
TILE = 128
GROUPS = TILE // 16
PAD = 8
EPS = 1e-05
VMEM_LIMIT = 58 * 2**20


def shifted(value, axis, steps):
    count = lax.axis_size(axis)
    initial, last = (max(0, -steps), min(count, count - steps))
    return lax.ppermute(value, axis, [(source, source + steps) for source in range(initial, last)])


def sublane_masks():
    sub = lax.broadcasted_iota(jnp.int32, (8, 128), 0)
    return [sub == i for i in range(8)]


def gather_rows(idx_ref, tables, dst_ref, tiles, masks):
    width = 128 * len(tables)

    def body(g, _):
        base_ref = idx_ref.at[pl.ds((g // GROUPS) * (K * TILE) + (g % GROUPS) * 16, (K - 1) * TILE + 16)]
        for k in range(K):
            both = [[] for _ in tables]
            for h in range(2):
                at = base_ref.at[pl.ds(k * TILE + h * 8, 8)]
                acc = [None for _ in tables]
                for i in range(8):
                    row = at[i]
                    for n, (table, base) in enumerate(tables):
                        v = table[pl.ds(row + (base + PAD - i), 8), :]
                        acc[n] = v if i == 0 else jnp.where(masks[i], v, acc[n])
                for n in range(len(tables)):
                    both[n].append(acc[n])
            for n in range(len(tables)):
                col = k * width + n * 128
                dst_ref[pl.ds(pl.multiple_of(g * 16, 16), 16), col : col + 128] = jnp.concatenate(
                    both[n], 0
                ).astype(jnp.bfloat16)
        return 0

    lax.fori_loop(0, tiles * GROUPS, body, 0)


def normed(h, gain):
    return h * lax.rsqrt(jnp.mean(h * h, axis=-1, keepdims=True) + EPS) * gain


def conv_kernel(
    second,
    idx_ref,
    counts_ref,
    lo_ref,
    mid_ref,
    hi_ref,
    w_in,
    gain_ref,
    *rest,
):
    if second:
        x_ref, wd_ref, gain_down_ref, place_ref, out_ref, down_ref, edge_ref, table, gathered, acc_ref, fine_ref, raw, placed = rest
    else:
        out_ref, table, gathered, acc_ref = rest
    step = pl.program_id(0)
    masks = sublane_masks()
    sub16 = lax.broadcasted_iota(jnp.int32, (8, 128), 0)

    @pl.when(step == 0)
    def _():
        table[:PAD, :] = jnp.zeros((PAD, 128), jnp.float32)
        table[pl.ds(PAD, 1024), :] = lo_ref[...].astype(jnp.float32)
        if second:
            table[pl.ds(PAD + 1024, 4096), :] = mid_ref[...].astype(jnp.float32)
        else:

            def masked(g, _):
                for i in range(8):
                    block = g * 16 + 2 * i
                    row = pl.multiple_of(block * 8, 16)
                    valid = jnp.concatenate([sub16 < counts_ref[block], sub16 < counts_ref[block + 1]], 0)
                    value = jnp.where(valid, mid_ref[pl.ds(row, 16), :].astype(jnp.float32), 0.0)
                    table[pl.ds(pl.multiple_of(row + (PAD + 1024), 8), 16), :] = value
                return 0

            lax.fori_loop(0, 32, masked, 0)
        table[pl.ds(PAD + 5120, 1024), :] = hi_ref[...].astype(jnp.float32)

    gather_rows(idx_ref, ((table, 0),), gathered, 8, masks)
    acc_ref[...] = jnp.dot(gathered[...], w_in[...], preferred_element_type=jnp.float32)

    def epilogue(tile, _):
        gain = gain_ref[...]
        for i in range(GROUPS):
            h = normed(acc_ref[pl.ds(pl.multiple_of(tile * TILE + i * 16, 16), 16), :], gain)
            row = pl.multiple_of(step * 1024 + tile * TILE + i * 16, 16)
            if second:
                h = x_ref[pl.ds(row, 16), :].astype(jnp.float32) + h
            block = step * 128 + tile * GROUPS * 2 + 2 * i
            valid = jnp.concatenate([sub16 < counts_ref[block], sub16 < counts_ref[block + 1]], 0)
            value = jnp.where(valid, jnp.maximum(h, 0.0), 0.0).astype(jnp.bfloat16)
            out_ref[pl.ds(row, 16), :] = value
            if second:
                fine_ref[pl.ds(row, 16), :] = value.astype(jnp.float32)
        return 0

    lax.fori_loop(0, 8, epilogue, 0)

    if second:

        @pl.when(step == 3)
        def _():

            def down(c, _):
                total = jnp.zeros((64, 256), jnp.float32)
                for j in range(8):
                    child = fine_ref[pl.ds(c * 512 + j, 64, stride=8), :].astype(jnp.bfloat16)
                    total += jnp.dot(child, wd_ref[j * 128 : (j + 1) * 128, :], preferred_element_type=jnp.float32)
                value = jnp.maximum(normed(total, gain_down_ref[...]), 0.0)
                row = pl.multiple_of(c * 64, 64)
                raw[pl.ds(row, 64), :] = value[:, :128]
                raw[pl.ds(row + 512, 64), :] = value[:, 128:]
                return 0

            lax.fori_loop(0, 8, down, 0)
            for n, row in enumerate((0, 448)):
                for h in range(2):
                    edge_ref[n * 64 : n * 64 + 64, h * 128 : h * 128 + 128] = raw[
                        h * 512 + row : h * 512 + row + 64, :
                    ].astype(jnp.bfloat16)
            placed[...] = jnp.zeros_like(placed)

            def put(g, _):
                for i in range(16):
                    at = place_ref[g * 16 + i]
                    placed[pl.ds(at, 1), :] = raw[pl.ds(g * 16 + i, 1), :]
                    placed[pl.ds(at + 520, 1), :] = raw[pl.ds(g * 16 + i + 512, 1), :]
                return 0

            lax.fori_loop(0, 32, put, 0)
            down_ref[:, :128] = placed[:512, :].astype(jnp.bfloat16)
            down_ref[:, 128:] = placed[520:1032, :].astype(jnp.bfloat16)


def whole(shape):
    return pl.BlockSpec(shape, lambda i: (0,) * len(shape))


def conv(second, idx, counts, lo, mid, hi, w, gain, *more, places=()):
    specs = [
        pl.BlockSpec((8 * K * TILE,), lambda i: (i,), memory_space=pltpu.SMEM),
        pl.BlockSpec(memory_space=pltpu.SMEM),
    ] + [whole(a.shape) for a in (lo, mid, hi, w, gain) + more]
    specs += [pl.BlockSpec(memory_space=pltpu.SMEM) for _ in places]
    out_shape = [jax.ShapeDtypeStruct((4096, 128), jnp.bfloat16)]
    scratch = [
        pltpu.VMEM((PAD + 6144 + 8, 128), jnp.float32),
        pltpu.VMEM((1024, K * 128), jnp.bfloat16),
        pltpu.VMEM((1024, 128), jnp.float32),
    ]
    if second:
        out_shape.append(jax.ShapeDtypeStruct((512, 256), jnp.bfloat16))
        out_shape.append(jax.ShapeDtypeStruct((128, 256), jnp.bfloat16))
        scratch.append(pltpu.VMEM((4096, 128), jnp.float32))
        scratch.append(pltpu.VMEM((1024, 128), jnp.float32))
        scratch.append(pltpu.VMEM((1040, 128), jnp.float32))
    return pl.pallas_call(
        functools.partial(conv_kernel, second),
        grid=(4,),
        in_specs=specs,
        out_specs=[whole(s.shape) for s in out_shape],
        out_shape=out_shape,
        scratch_shapes=scratch,
        name="conv_second" if second else "conv_first",
        compiler_params=pltpu.CompilerParams(vmem_limit_bytes=VMEM_LIMIT),
    )(idx, counts, lo, mid, hi, w, gain, *more, *places)


HALF = 2048 + 16
NOWHERE = PAD + 2048
REACH = 640


def ring(axis):
    me, count = lax.axis_index(axis), lax.axis_size(axis)
    return lax.rem(me + 1, count), lax.rem(me + count - 1, count)


def greet(partners):
    barrier = pltpu.get_barrier_semaphore()
    for partner in partners:
        pl.semaphore_signal(barrier, inc=1, device_id=partner, device_id_type=pl.DeviceIdType.MESH)
    pl.semaphore_wait(barrier, len(partners))


def sender(send_sem, recv_sem):
    count = [0]

    def send(src, dst, partner):
        n = count[0]
        count[0] += 1
        copy = pltpu.make_async_remote_copy(
            src_ref=src,
            dst_ref=dst,
            send_sem=send_sem.at[n],
            recv_sem=recv_sem.at[n],
            device_id=partner,
            device_id_type=pl.DeviceIdType.MESH,
        )
        copy.start()
        return copy

    return send


def halo_kernel(field_ref, lo_ref, hi_ref, send_sem, recv_sem):
    tile = lax.axis_index("tile")
    above, below = ring("morton")
    greet([(tile, above), (tile, below)])
    send = sender(send_sem, recv_sem)
    copies = [
        send(field_ref.at[pl.ds(3072, 1024)], lo_ref, (tile, above)),
        send(field_ref.at[pl.ds(0, 1024)], hi_ref, (tile, below)),
    ]
    for copy in copies:
        copy.wait()


def halo_of(field):
    return pl.pallas_call(
        halo_kernel,
        in_specs=[pl.BlockSpec(memory_space=pl.ANY)],
        out_specs=[pl.BlockSpec(memory_space=pl.ANY)] * 2,
        out_shape=[jax.ShapeDtypeStruct((1024, 128), jnp.bfloat16)] * 2,
        scratch_shapes=[pltpu.SemaphoreType.DMA((2,)), pltpu.SemaphoreType.DMA((2,))],
        name="halo",
        compiler_params=pltpu.CompilerParams(collective_id=1, has_side_effects=True),
    )(field)


def exchange_kernel(rows_ref, edge_ref, codes_ref, pool_ref, places_ref, send_sem, recv_sem, local_sem):
    tile, me = lax.axis_index("tile"), lax.axis_index("morton")
    right, left = ring("tile")
    above, below = ring("morton")
    opposite = lax.rem(tile + 2, lax.axis_size("tile"))
    tiles = (tile, right, left, opposite)
    greet([(right, me), (left, me)] + [(t, m) for t in tiles for m in (above, below)])

    send = sender(send_sem, recv_sem)
    first, last = pl.ds(0, 256), pl.ds(256, 256)
    from_below, from_above = pl.ds(512, 64), pl.ds(576, 64)
    right_first = send(rows_ref.at[first], pool_ref.at[tile, first], (right, me))
    left_last = send(rows_ref.at[last], pool_ref.at[tile, last], (left, me))
    handed = {}
    for n, t in enumerate((right, left, tile)):
        handed[n, 0] = send(edge_ref.at[pl.ds(64, 64)], pool_ref.at[tile, from_below], (t, above))
        handed[n, 1] = send(edge_ref.at[pl.ds(0, 64)], pool_ref.at[tile, from_above], (t, below))
    others = [send(rows_ref.at[last], pool_ref.at[tile, last], (right, me))]
    others.append(send(rows_ref.at[first], pool_ref.at[tile, first], (left, me)))
    for t in tiles:
        others.append(send(codes_ref, places_ref.at[0, tile], (t, above)))
        others.append(send(codes_ref, places_ref.at[1, tile], (t, below)))
    own = pltpu.make_async_copy(rows_ref, pool_ref.at[tile, pl.ds(0, 512)], local_sem)
    own.start()

    relays = ((right_first, left, first, right), (left_last, right, last, left))
    relays += ((handed[0, 0], left, from_below, right), (handed[1, 1], right, from_above, left))
    passed = []
    for copy, source, part, target in relays:
        copy.wait_recv()
        passed.append(send(pool_ref.at[source, part], pool_ref.at[source, part], (target, me)))
    for copy, _, _, _ in relays:
        copy.wait_send()
    own.wait()
    for copy in [handed[0, 1], handed[1, 0], handed[2, 0], handed[2, 1]] + others + passed:
        copy.wait()


def exchange(rows, edges, codes):
    return pl.pallas_call(
        exchange_kernel,
        in_specs=[pl.BlockSpec(memory_space=pl.ANY)] * 3,
        out_specs=[pl.BlockSpec(memory_space=pl.ANY)] * 2,
        out_shape=[
            jax.ShapeDtypeStruct((4, REACH, 256), jnp.bfloat16),
            jax.ShapeDtypeStruct((2, 4, 8, 128), jnp.int32),
        ],
        scratch_shapes=[
            pltpu.SemaphoreType.DMA((22,)),
            pltpu.SemaphoreType.DMA((22,)),
            pltpu.SemaphoreType.DMA,
        ],
        name="exchange",
        compiler_params=pltpu.CompilerParams(collective_id=0, has_side_effects=True),
    )(rows, edges, codes)


def coarse_kernel(idx_ref, places_ref, pool_ref, w_in, gain_ref, out_ref, table, source, gathered, acc_ref):
    masks = sublane_masks()
    table[:PAD, :] = jnp.zeros((PAD, 128), jnp.float32)
    table[HALF : HALF + PAD, :] = jnp.zeros((PAD, 128), jnp.float32)

    def tile_rows(t, _):
        row = pl.multiple_of(PAD + t * 512, 8)
        for h in range(2):
            cols = slice(h * 128, h * 128 + 128)
            table[pl.ds(row + h * HALF, 512), :] = pool_ref[t, :512, cols].astype(jnp.float32)
            source[pl.ds((t * 2 + h) * 128, 128), :] = pool_ref[t, 512:, cols].astype(jnp.float32)
        return 0

    lax.fori_loop(0, 4, tile_rows, 0)

    def handed(t, _):
        for kind in range(2):
            for i in range(64):
                at = places_ref[kind, t, 0, kind * 64 + i]
                row = t * 256 + kind * 64 + i
                table[pl.ds(at, 1), :] = source[pl.ds(row, 1), :]
                table[pl.ds(at + HALF, 1), :] = source[pl.ds(row + 128, 1), :]
        return 0

    lax.fori_loop(0, 4, handed, 0)
    gather_rows(idx_ref, ((table, 0), (table, HALF)), gathered, 4, masks)
    acc_ref[...] = jnp.dot(gathered[...], w_in[...], preferred_element_type=jnp.float32)
    first = PAD + 512 * lax.axis_index("tile")

    def epilogue(tile, _):
        for i in range(GROUPS):
            row = pl.multiple_of(tile * TILE + i * 16, 16)
            h = normed(acc_ref[pl.ds(row, 16), :], gain_ref[...])
            at = pl.multiple_of(first + row, 8)
            own = jnp.concatenate([table[pl.ds(at, 16), :], table[pl.ds(at + HALF, 16), :]], 1)
            out_ref[pl.ds(row, 16), :] = jnp.maximum(own + h, 0.0).astype(jnp.bfloat16)
        return 0

    lax.fori_loop(0, 4, epilogue, 0)


def coarse(idx, places, pool, w, gain):
    return pl.pallas_call(
        coarse_kernel,
        in_specs=[pl.BlockSpec(memory_space=pltpu.SMEM)] * 2 + [pl.BlockSpec(memory_space=pltpu.VMEM)] * 3,
        out_specs=pl.BlockSpec(memory_space=pltpu.VMEM),
        out_shape=jax.ShapeDtypeStruct((512, 256), jnp.bfloat16),
        scratch_shapes=[
            pltpu.VMEM((2 * HALF, 128), jnp.float32),
            pltpu.VMEM((1024, 128), jnp.float32),
            pltpu.VMEM((512, K * 256), jnp.bfloat16),
            pltpu.VMEM((512, 256), jnp.float32),
        ],
        name="coarse",
        compiler_params=pltpu.CompilerParams(vmem_limit_bytes=VMEM_LIMIT),
    )(idx, places, pool, w, gain)


def by_tiles(index):
    rows = index.shape[1]
    return index.reshape(K, rows // TILE, TILE).transpose(1, 0, 2).reshape(-1)


def shards(
    features,
    neighbours,
    counts,
    owner,
    slot,
    coarse_neighbours,
    w_first,
    w_second,
    w_down,
    w_coarse,
    gain_first,
    gain_second,
    gain_down,
    gain_coarse,
):
    lane_ids = jnp.arange(8, dtype=jnp.int32)

    def masked(first):
        valid = lane_ids[None, :] < counts[0, first : first + 128, None]
        rows = features[0, 8 * first : 8 * first + 1024].reshape(128, 8, 128)
        return jnp.where(valid[:, :, None], rows, 0).astype(jnp.bfloat16).reshape(1024, 128)

    lo, hi = shifted(masked(384), "morton", 1), shifted(masked(0), "morton", -1)
    by_offset = neighbours[0].T
    local = by_offset + jnp.arange(4096, dtype=jnp.int32)[None, :]
    idx = by_tiles(jnp.where(by_offset < 0, -1, local))
    coarse_idx = by_tiles(coarse_neighbours[0].T)

    me = lax.axis_index("morton")
    destination = owner[0]
    at = PAD + 512 * lax.axis_index("tile") + slot[0]

    def handed(to):
        return jnp.where(destination == to, at, NOWHERE)

    edges = jnp.concatenate([handed(me + 1)[448:], handed(me - 1)[:64]])
    codes = jnp.broadcast_to(edges[None], (8, 128))
    kept = jnp.where(destination == me, slot[0], 512)

    (act,) = conv(False, idx, counts[0], lo, features[0], hi, w_first, gain_first[None])
    lo, hi = halo_of(act)
    fine, rows, edge_rows = conv(
        True, idx, counts[0], lo, act, hi, w_second, gain_second[None], features[0], w_down, gain_down[None], places=(kept,)
    )
    pool, places = exchange(rows, edge_rows, codes)
    out = coarse(coarse_idx, places, pool, w_coarse, gain_coarse[None])
    return fine[None], out[None]


def solution(mesh):
    split = P("tile", "morton", None)
    flat = P("tile", "morton")
    in_specs = (split, split, flat, flat, flat, split) + (P(),) * 8
    return jax.shard_map(shards, mesh=mesh, in_specs=in_specs, out_specs=(split, split), check_vma=False)
```

```python
import functools

import jax
import jax.numpy as jnp
from jax import lax
from jax.experimental import pallas as pl
from jax.experimental.pallas import tpu as pltpu
from jax.sharding import PartitionSpec as P

K = 27
TILE = 128
GROUPS = TILE // 16
PAD = 8
PLAN = 1280
LISTED = 1056
MOSTLY = 640
EPS = 1e-05
VMEM_LIMIT = 58 * 2**20


def shifted(value, axis, steps):
    count = lax.axis_size(axis)
    initial, last = (max(0, -steps), min(count, count - steps))
    return lax.ppermute(value, axis, [(source, source + steps) for source in range(initial, last)])


def sublane_masks():
    sub = lax.broadcasted_iota(jnp.int32, (8, 128), 0)
    return [sub == i for i in range(8)]


def gather_rows(idx_ref, tables, dst_ref, tiles, masks):
    width = 128 * len(tables)

    def body(step, _):
        for part in range(2):
            g = step * 2 + part
            base_ref = idx_ref.at[pl.ds((step // 4) * (K * TILE) + (step % 4) * 32, (K - 1) * TILE + 32)]
            for k in range(K):
                both = [[] for _ in tables]
                for h in range(2):
                    first = k * TILE + part * 16 + h * 8
                    lead = 8 if first else 0
                    at = base_ref.at[pl.ds(first - lead, 8 + lead)]
                    acc = [None for _ in tables]
                    for i in range(8):
                        row = at[lead + i]
                        for n, (table, base) in enumerate(tables):
                            v = table[pl.ds(row + (base + PAD - i), 8), :]
                            acc[n] = v if i == 0 else jnp.where(masks[i], v, acc[n])
                    for n in range(len(tables)):
                        both[n].append(acc[n])
                for n in range(len(tables)):
                    col = k * width + n * 128
                    dst_ref[pl.ds(pl.multiple_of(g * 16, 16), 16), col : col + 128] = jnp.concatenate(
                        both[n], 0
                    ).astype(jnp.bfloat16)
        return 0

    lax.fori_loop(0, tiles * 4, body, 0)


def gather_listed(idx_ref, plan_ref, first, groups, table, dst_ref, masks):
    def body(g, _):
        both = []
        for h in range(2):
            listed = plan_ref.at[pl.ds(first + g * 16 + h * 8, 8)]
            at = [idx_ref.at[pl.ds(listed[i], (K - 1) * TILE + 1)] for i in range(8)]
            both.append([])
            for k in range(K):
                acc = None
                for i in range(8):
                    v = table[pl.ds(at[i][k * TILE] + (PAD - i), 8), :]
                    acc = v if i == 0 else jnp.where(masks[i], v, acc)
                both[h].append(acc)
                if h:
                    dst_ref[pl.ds(pl.multiple_of(g * 16, 16), 16), k * 128 : k * 128 + 128] = jnp.concatenate(
                        [both[0][k], acc], 0
                    ).astype(jnp.bfloat16)
        return 0

    lax.fori_loop(0, groups, body, 0)


def normed(h, gain):
    return h * lax.rsqrt(jnp.mean(h * h, axis=-1, keepdims=True) + EPS) * gain


def conv_kernel(
    second,
    idx_ref,
    plan_ref,
    counts_ref,
    lo_ref,
    mid_ref,
    hi_ref,
    w_in,
    gain_ref,
    *rest,
):
    if second:
        x_ref, wd_ref, gain_down_ref, place_ref, out_ref, down_ref, edge_ref, table, gathered, acc_ref, fine_ref, raw, placed = rest
    else:
        out_ref, table, gathered, acc_ref = rest
    step = pl.program_id(0)
    masks = sublane_masks()
    sub16 = lax.broadcasted_iota(jnp.int32, (8, 128), 0)

    @pl.when(step == 0)
    def _():
        table[:PAD, :] = jnp.zeros((PAD, 128), jnp.float32)
        table[pl.ds(PAD, 1024), :] = lo_ref[...].astype(jnp.float32)
        if second:
            table[pl.ds(PAD + 1024, 4096), :] = mid_ref[...].astype(jnp.float32)
        else:

            def masked(g, _):
                for i in range(8):
                    block = g * 16 + 2 * i
                    row = pl.multiple_of(block * 8, 16)
                    valid = jnp.concatenate([sub16 < counts_ref[block], sub16 < counts_ref[block + 1]], 0)
                    value = jnp.where(valid, mid_ref[pl.ds(row, 16), :].astype(jnp.float32), 0.0)
                    table[pl.ds(pl.multiple_of(row + (PAD + 1024), 8), 16), :] = value
                return 0

            lax.fori_loop(0, 32, masked, 0)
        table[pl.ds(PAD + 5120, 1024), :] = hi_ref[...].astype(jnp.float32)

    plan = step * PLAN
    total = plan_ref[plan + LISTED + 128]
    gather_listed(idx_ref, plan_ref, plan, (total + 15) // 16, table, gathered, masks)
    acc_ref[:MOSTLY, :] = jnp.dot(gathered[:MOSTLY, :], w_in[...], preferred_element_type=jnp.float32)

    @pl.when(total > MOSTLY)
    def _():
        acc_ref[MOSTLY:1024, :] = jnp.dot(gathered[MOSTLY:, :], w_in[...], preferred_element_type=jnp.float32)

    def epilogue(tile, _):
        gain = gain_ref[...]
        for i in range(GROUPS):
            start = plan_ref.at[pl.ds(plan + LISTED + tile * GROUPS * 2 + 2 * i, 2)]
            h = normed(jnp.concatenate([acc_ref[pl.ds(start[0], 8), :], acc_ref[pl.ds(start[1], 8), :]], 0), gain)
            row = pl.multiple_of(step * 1024 + tile * TILE + i * 16, 16)
            if second:
                h = x_ref[pl.ds(row, 16), :].astype(jnp.float32) + h
            block = step * 128 + tile * GROUPS * 2 + 2 * i
            valid = jnp.concatenate([sub16 < counts_ref[block], sub16 < counts_ref[block + 1]], 0)
            value = jnp.where(valid, jnp.maximum(h, 0.0), 0.0).astype(jnp.bfloat16)
            out_ref[pl.ds(row, 16), :] = value
            if second:
                fine_ref[pl.ds(row, 16), :] = value.astype(jnp.float32)
        return 0

    lax.fori_loop(0, 8, epilogue, 0)

    if second:

        @pl.when(step == 3)
        def _():

            def down(c, _):
                total = jnp.zeros((64, 256), jnp.float32)
                for j in range(8):
                    child = fine_ref[pl.ds(c * 512 + j, 64, stride=8), :].astype(jnp.bfloat16)
                    total += jnp.dot(child, wd_ref[j * 128 : (j + 1) * 128, :], preferred_element_type=jnp.float32)
                value = jnp.maximum(normed(total, gain_down_ref[...]), 0.0)
                row = pl.multiple_of(c * 64, 64)
                raw[pl.ds(row, 64), :] = value[:, :128]
                raw[pl.ds(row + 512, 64), :] = value[:, 128:]
                return 0

            lax.fori_loop(0, 8, down, 0)
            for n, row in enumerate((0, 448)):
                for h in range(2):
                    edge_ref[n * 64 : n * 64 + 64, h * 128 : h * 128 + 128] = raw[
                        h * 512 + row : h * 512 + row + 64, :
                    ].astype(jnp.bfloat16)
            placed[...] = jnp.zeros_like(placed)

            def put(g, _):
                for i in range(16):
                    at = place_ref[g * 16 + i]
                    placed[pl.ds(at, 1), :] = raw[pl.ds(g * 16 + i, 1), :]
                    placed[pl.ds(at + 520, 1), :] = raw[pl.ds(g * 16 + i + 512, 1), :]
                return 0

            lax.fori_loop(0, 32, put, 0)
            down_ref[:, :128] = placed[:512, :].astype(jnp.bfloat16)
            down_ref[:, 128:] = placed[520:1032, :].astype(jnp.bfloat16)


def whole(shape):
    return pl.BlockSpec(shape, lambda i: (0,) * len(shape))


def conv(second, idx, plan, counts, lo, mid, hi, w, gain, *more, places=()):
    specs = [
        pl.BlockSpec((8 * K * TILE,), lambda i: (i,), memory_space=pltpu.SMEM),
        pl.BlockSpec(memory_space=pltpu.SMEM),
        pl.BlockSpec(memory_space=pltpu.SMEM),
    ] + [whole(a.shape) for a in (lo, mid, hi, w, gain) + more]
    specs += [pl.BlockSpec(memory_space=pltpu.SMEM) for _ in places]
    out_shape = [jax.ShapeDtypeStruct((4096, 128), jnp.bfloat16)]
    scratch = [
        pltpu.VMEM((PAD + 6144 + 8, 128), jnp.float32),
        pltpu.VMEM((1024, K * 128), jnp.bfloat16),
        pltpu.VMEM((1024 + 8, 128), jnp.float32),
    ]
    if second:
        out_shape.append(jax.ShapeDtypeStruct((512, 256), jnp.bfloat16))
        out_shape.append(jax.ShapeDtypeStruct((128, 256), jnp.bfloat16))
        scratch.append(pltpu.VMEM((4096, 128), jnp.float32))
        scratch.append(pltpu.VMEM((1024, 128), jnp.float32))
        scratch.append(pltpu.VMEM((1040, 128), jnp.float32))
    return pl.pallas_call(
        functools.partial(conv_kernel, second),
        grid=(4,),
        in_specs=specs,
        out_specs=[whole(s.shape) for s in out_shape],
        out_shape=out_shape,
        scratch_shapes=scratch,
        name="conv_second" if second else "conv_first",
        compiler_params=pltpu.CompilerParams(vmem_limit_bytes=VMEM_LIMIT),
    )(idx, plan, counts, lo, mid, hi, w, gain, *more, *places)


HALF = 2048 + 16
NOWHERE = PAD + 2048
REACH = 640


def ring(axis):
    me, count = lax.axis_index(axis), lax.axis_size(axis)
    return lax.rem(me + 1, count), lax.rem(me + count - 1, count)


def greet(partners):
    barrier = pltpu.get_barrier_semaphore()
    for partner in partners:
        pl.semaphore_signal(barrier, inc=1, device_id=partner, device_id_type=pl.DeviceIdType.MESH)
    pl.semaphore_wait(barrier, len(partners))


def sender(send_sem, recv_sem):
    count = [0]

    def send(src, dst, partner):
        n = count[0]
        count[0] += 1
        copy = pltpu.make_async_remote_copy(
            src_ref=src,
            dst_ref=dst,
            send_sem=send_sem.at[n],
            recv_sem=recv_sem.at[n],
            device_id=partner,
            device_id_type=pl.DeviceIdType.MESH,
        )
        copy.start()
        return copy

    return send


def halo_kernel(field_ref, lo_ref, hi_ref, send_sem, recv_sem):
    tile = lax.axis_index("tile")
    above, below = ring("morton")
    greet([(tile, above), (tile, below)])
    send = sender(send_sem, recv_sem)
    copies = [
        send(field_ref.at[pl.ds(3072, 1024)], lo_ref, (tile, above)),
        send(field_ref.at[pl.ds(0, 1024)], hi_ref, (tile, below)),
    ]
    for copy in copies:
        copy.wait()


def halo_of(field):
    return pl.pallas_call(
        halo_kernel,
        in_specs=[pl.BlockSpec(memory_space=pl.ANY)],
        out_specs=[pl.BlockSpec(memory_space=pl.ANY)] * 2,
        out_shape=[jax.ShapeDtypeStruct((1024, 128), jnp.bfloat16)] * 2,
        scratch_shapes=[pltpu.SemaphoreType.DMA((2,)), pltpu.SemaphoreType.DMA((2,))],
        name="halo",
        compiler_params=pltpu.CompilerParams(collective_id=1, has_side_effects=True),
    )(field)


def exchange_kernel(rows_ref, edge_ref, codes_ref, pool_ref, places_ref, send_sem, recv_sem, local_sem):
    tile, me = lax.axis_index("tile"), lax.axis_index("morton")
    right, left = ring("tile")
    above, below = ring("morton")
    opposite = lax.rem(tile + 2, lax.axis_size("tile"))
    tiles = (tile, right, left, opposite)
    greet([(right, me), (left, me)] + [(t, m) for t in tiles for m in (above, below)])

    send = sender(send_sem, recv_sem)
    first, last = pl.ds(0, 256), pl.ds(256, 256)
    from_below, from_above = pl.ds(512, 64), pl.ds(576, 64)
    right_first = send(rows_ref.at[first], pool_ref.at[tile, first], (right, me))
    left_last = send(rows_ref.at[last], pool_ref.at[tile, last], (left, me))
    handed = {}
    for n, t in enumerate((right, left, tile)):
        handed[n, 0] = send(edge_ref.at[pl.ds(64, 64)], pool_ref.at[tile, from_below], (t, above))
        handed[n, 1] = send(edge_ref.at[pl.ds(0, 64)], pool_ref.at[tile, from_above], (t, below))
    others = [send(rows_ref.at[last], pool_ref.at[tile, last], (right, me))]
    others.append(send(rows_ref.at[first], pool_ref.at[tile, first], (left, me)))
    for t in tiles:
        others.append(send(codes_ref, places_ref.at[0, tile], (t, above)))
        others.append(send(codes_ref, places_ref.at[1, tile], (t, below)))
    own = pltpu.make_async_copy(rows_ref, pool_ref.at[tile, pl.ds(0, 512)], local_sem)
    own.start()

    relays = ((right_first, left, first, right), (left_last, right, last, left))
    relays += ((handed[0, 0], left, from_below, right), (handed[1, 1], right, from_above, left))
    passed = []
    for copy, source, part, target in relays:
        copy.wait_recv()
        passed.append(send(pool_ref.at[source, part], pool_ref.at[source, part], (target, me)))
    for copy, _, _, _ in relays:
        copy.wait_send()
    own.wait()
    for copy in [handed[0, 1], handed[1, 0], handed[2, 0], handed[2, 1]] + others + passed:
        copy.wait()


def exchange(rows, edges, codes):
    return pl.pallas_call(
        exchange_kernel,
        in_specs=[pl.BlockSpec(memory_space=pl.ANY)] * 3,
        out_specs=[pl.BlockSpec(memory_space=pl.ANY)] * 2,
        out_shape=[
            jax.ShapeDtypeStruct((4, REACH, 256), jnp.bfloat16),
            jax.ShapeDtypeStruct((2, 4, 8, 128), jnp.int32),
        ],
        scratch_shapes=[
            pltpu.SemaphoreType.DMA((22,)),
            pltpu.SemaphoreType.DMA((22,)),
            pltpu.SemaphoreType.DMA,
        ],
        name="exchange",
        compiler_params=pltpu.CompilerParams(collective_id=0, has_side_effects=True),
    )(rows, edges, codes)


def coarse_kernel(idx_ref, places_ref, pool_ref, w_in, gain_ref, out_ref, table, source, gathered, acc_ref):
    masks = sublane_masks()
    table[:PAD, :] = jnp.zeros((PAD, 128), jnp.float32)
    table[HALF : HALF + PAD, :] = jnp.zeros((PAD, 128), jnp.float32)

    def tile_rows(t, _):
        row = pl.multiple_of(PAD + t * 512, 8)
        for h in range(2):
            cols = slice(h * 128, h * 128 + 128)
            table[pl.ds(row + h * HALF, 512), :] = pool_ref[t, :512, cols].astype(jnp.float32)
            source[pl.ds((t * 2 + h) * 128, 128), :] = pool_ref[t, 512:, cols].astype(jnp.float32)
        return 0

    lax.fori_loop(0, 4, tile_rows, 0)

    def handed(t, _):
        for kind in range(2):
            for i in range(64):
                at = places_ref[kind, t, 0, kind * 64 + i]
                row = t * 256 + kind * 64 + i
                table[pl.ds(at, 1), :] = source[pl.ds(row, 1), :]
                table[pl.ds(at + HALF, 1), :] = source[pl.ds(row + 128, 1), :]
        return 0

    lax.fori_loop(0, 4, handed, 0)
    gather_rows(idx_ref, ((table, 0), (table, HALF)), gathered, 4, masks)
    acc_ref[...] = jnp.dot(gathered[...], w_in[...], preferred_element_type=jnp.float32)
    first = PAD + 512 * lax.axis_index("tile")

    def epilogue(tile, _):
        for i in range(GROUPS):
            row = pl.multiple_of(tile * TILE + i * 16, 16)
            h = normed(acc_ref[pl.ds(row, 16), :], gain_ref[...])
            at = pl.multiple_of(first + row, 8)
            own = jnp.concatenate([table[pl.ds(at, 16), :], table[pl.ds(at + HALF, 16), :]], 1)
            out_ref[pl.ds(row, 16), :] = jnp.maximum(own + h, 0.0).astype(jnp.bfloat16)
        return 0

    lax.fori_loop(0, 4, epilogue, 0)


def coarse(idx, places, pool, w, gain):
    return pl.pallas_call(
        coarse_kernel,
        in_specs=[pl.BlockSpec(memory_space=pltpu.SMEM)] * 2 + [pl.BlockSpec(memory_space=pltpu.VMEM)] * 3,
        out_specs=pl.BlockSpec(memory_space=pltpu.VMEM),
        out_shape=jax.ShapeDtypeStruct((512, 256), jnp.bfloat16),
        scratch_shapes=[
            pltpu.VMEM((2 * HALF, 128), jnp.float32),
            pltpu.VMEM((1024, 128), jnp.float32),
            pltpu.VMEM((512, K * 256), jnp.bfloat16),
            pltpu.VMEM((512, 256), jnp.float32),
        ],
        name="coarse",
        compiler_params=pltpu.CompilerParams(vmem_limit_bytes=VMEM_LIMIT),
    )(idx, places, pool, w, gain)


def by_tiles(index):
    rows = index.shape[1]
    return index.reshape(K, rows // TILE, TILE).transpose(1, 0, 2).reshape(-1)


def plan_of(counts):
    held = counts.reshape(4, 128)
    block = jnp.arange(128, dtype=jnp.int32)
    ends = jnp.sum(jnp.where(block[None, :] <= block[:, None], held[:, None, :], 0), axis=-1)
    place = jnp.arange(LISTED, dtype=jnp.int32)
    past = ends[:, None, :] <= place[None, :, None]
    at = jnp.sum(past.astype(jnp.int32), axis=-1)
    start = jnp.max(jnp.where(past, ends[:, None, :], 0), axis=-1)
    entry = (at // 16) * (K * TILE) + (at % 16) * 8 + place[None, :] - start
    listed = jnp.where(at < 128, entry, 0)
    rest = jnp.broadcast_to(ends[:, 127:], (4, PLAN - LISTED - 128))
    return jnp.concatenate([listed, ends - held, rest], axis=1).reshape(-1)


def shards(
    features,
    neighbours,
    counts,
    owner,
    slot,
    coarse_neighbours,
    w_first,
    w_second,
    w_down,
    w_coarse,
    gain_first,
    gain_second,
    gain_down,
    gain_coarse,
):
    lane_ids = jnp.arange(8, dtype=jnp.int32)

    def masked(first):
        valid = lane_ids[None, :] < counts[0, first : first + 128, None]
        rows = features[0, 8 * first : 8 * first + 1024].reshape(128, 8, 128)
        return jnp.where(valid[:, :, None], rows, 0).astype(jnp.bfloat16).reshape(1024, 128)

    lo, hi = shifted(masked(384), "morton", 1), shifted(masked(0), "morton", -1)
    by_offset = neighbours[0].T
    local = by_offset + jnp.arange(4096, dtype=jnp.int32)[None, :]
    idx = by_tiles(jnp.where(by_offset < 0, -1, local))
    plan = plan_of(counts[0])
    coarse_idx = by_tiles(coarse_neighbours[0].T)

    me = lax.axis_index("morton")
    destination = owner[0]
    at = PAD + 512 * lax.axis_index("tile") + slot[0]

    def handed(to):
        return jnp.where(destination == to, at, NOWHERE)

    edges = jnp.concatenate([handed(me + 1)[448:], handed(me - 1)[:64]])
    codes = jnp.broadcast_to(edges[None], (8, 128))
    kept = jnp.where(destination == me, slot[0], 512)

    (act,) = conv(False, idx, plan, counts[0], lo, features[0], hi, w_first, gain_first[None])
    lo, hi = halo_of(act)
    fine, rows, edge_rows = conv(
        True, idx, plan, counts[0], lo, act, hi, w_second, gain_second[None], features[0], w_down, gain_down[None], places=(kept,)
    )
    pool, places = exchange(rows, edge_rows, codes)
    out = coarse(coarse_idx, places, pool, w_coarse, gain_coarse[None])
    return fine[None], out[None]


def solution(mesh):
    split = P("tile", "morton", None)
    flat = P("tile", "morton")
    in_specs = (split, split, flat, flat, flat, split) + (P(),) * 8
    return jax.shard_map(shards, mesh=mesh, in_specs=in_specs, out_specs=(split, split), check_vma=False)
```

```python
import functools

import jax
import jax.numpy as jnp
from jax import lax
from jax.experimental import pallas as pl
from jax.experimental.pallas import tpu as pltpu
from jax.sharding import PartitionSpec as P

K = 27
SELF = 13
OTHERS = tuple(k for k in range(K) if k != SELF)
TILE = 128
GROUPS = TILE // 16
PAD = 8
PLAN = 1280
LISTED = 1056
MOSTLY = 640
EPS = 1e-05
VMEM_LIMIT = 58 * 2**20


def shifted(value, axis, steps):
    count = lax.axis_size(axis)
    initial, last = (max(0, -steps), min(count, count - steps))
    return lax.ppermute(value, axis, [(source, source + steps) for source in range(initial, last)])


def sublane_masks():
    sub = lax.broadcasted_iota(jnp.int32, (8, 128), 0)
    return [sub == i for i in range(8)]


def gather_rows(idx_ref, tables, dst_ref, tiles, masks):
    width = 128 * len(tables)

    def body(step, _):
        for part in range(2):
            g = step * 2 + part
            base_ref = idx_ref.at[pl.ds((step // 4) * (K * TILE) + (step % 4) * 32, (K - 1) * TILE + 32)]
            for k in range(K):
                both = [[] for _ in tables]
                for h in range(2):
                    first = k * TILE + part * 16 + h * 8
                    lead = 8 if first else 0
                    at = base_ref.at[pl.ds(first - lead, 8 + lead)]
                    acc = [None for _ in tables]
                    for i in range(8):
                        row = at[lead + i]
                        for n, (table, base) in enumerate(tables):
                            v = table[pl.ds(row + (base + PAD - i), 8), :]
                            acc[n] = v if i == 0 else jnp.where(masks[i], v, acc[n])
                    for n in range(len(tables)):
                        both[n].append(acc[n])
                for n in range(len(tables)):
                    col = k * width + n * 128
                    dst_ref[pl.ds(pl.multiple_of(g * 16, 16), 16), col : col + 128] = jnp.concatenate(
                        both[n], 0
                    ).astype(jnp.bfloat16)
        return 0

    lax.fori_loop(0, tiles * 4, body, 0)


def gather_listed(idx_ref, plan_ref, first, groups, table, dst_ref, masks):
    def body(g, _):
        both = []
        for h in range(2):
            listed = plan_ref.at[pl.ds(first + g * 16 + h * 8, 8)]
            at = [idx_ref.at[pl.ds(listed[i], (K - 1) * TILE + 1)] for i in range(8)]
            both.append([])
            for n, k in enumerate(OTHERS):
                acc = None
                for i in range(8):
                    v = table[pl.ds(at[i][k * TILE] + (PAD - i), 8), :]
                    acc = v if i == 0 else jnp.where(masks[i], v, acc)
                both[h].append(acc)
                if h:
                    dst_ref[pl.ds(pl.multiple_of(g * 16, 16), 16), n * 128 : n * 128 + 128] = jnp.concatenate(
                        [both[0][n], acc], 0
                    ).astype(jnp.bfloat16)
        return 0

    lax.fori_loop(0, groups, body, 0)


def normed(h, gain):
    return h * lax.rsqrt(jnp.mean(h * h, axis=-1, keepdims=True) + EPS) * gain


def conv_kernel(
    second,
    idx_ref,
    plan_ref,
    counts_ref,
    lo_ref,
    mid_ref,
    hi_ref,
    w_in,
    gain_ref,
    *rest,
):
    if second:
        x_ref, wd_ref, gain_down_ref, place_ref, out_ref, down_ref, edge_ref, table, gathered, acc_ref, w_ref, self_ref, fine_ref, raw, placed = rest
    else:
        out_ref, table, gathered, acc_ref, w_ref, self_ref = rest
    step = pl.program_id(0)
    masks = sublane_masks()
    sub16 = lax.broadcasted_iota(jnp.int32, (8, 128), 0)

    @pl.when(step == 0)
    def _():
        table[:PAD, :] = jnp.zeros((PAD, 128), jnp.float32)
        w_ref[: SELF * 128, :] = w_in[: SELF * 128, :]
        w_ref[SELF * 128 :, :] = w_in[(SELF + 1) * 128 :, :]
        table[pl.ds(PAD, 1024), :] = lo_ref[...].astype(jnp.float32)
        if second:
            table[pl.ds(PAD + 1024, 4096), :] = mid_ref[...].astype(jnp.float32)
        else:

            def masked(g, _):
                for i in range(8):
                    block = g * 16 + 2 * i
                    row = pl.multiple_of(block * 8, 16)
                    valid = jnp.concatenate([sub16 < counts_ref[block], sub16 < counts_ref[block + 1]], 0)
                    value = jnp.where(valid, mid_ref[pl.ds(row, 16), :].astype(jnp.float32), 0.0)
                    table[pl.ds(pl.multiple_of(row + (PAD + 1024), 8), 16), :] = value
                return 0

            lax.fori_loop(0, 32, masked, 0)
        table[pl.ds(PAD + 5120, 1024), :] = hi_ref[...].astype(jnp.float32)

    plan = step * PLAN
    total = plan_ref[plan + LISTED + 128]
    gather_listed(idx_ref, plan_ref, plan, (total + 15) // 16, table, gathered, masks)
    own = mid_ref[pl.ds(pl.multiple_of(step * 1024, 1024), 1024), :]
    self_ref[...] = jnp.dot(own, w_in[SELF * 128 : (SELF + 1) * 128, :], preferred_element_type=jnp.float32)
    acc_ref[:MOSTLY, :] = jnp.dot(gathered[:MOSTLY, :], w_ref[...], preferred_element_type=jnp.float32)

    @pl.when(total > MOSTLY)
    def _():
        acc_ref[MOSTLY:1024, :] = jnp.dot(gathered[MOSTLY:, :], w_ref[...], preferred_element_type=jnp.float32)

    def epilogue(tile, _):
        gain = gain_ref[...]
        for i in range(GROUPS):
            start = plan_ref.at[pl.ds(plan + LISTED + tile * GROUPS * 2 + 2 * i, 2)]
            h = jnp.concatenate([acc_ref[pl.ds(start[0], 8), :], acc_ref[pl.ds(start[1], 8), :]], 0)
            h = normed(h + self_ref[pl.ds(pl.multiple_of(tile * TILE + i * 16, 16), 16), :], gain)
            row = pl.multiple_of(step * 1024 + tile * TILE + i * 16, 16)
            if second:
                h = x_ref[pl.ds(row, 16), :].astype(jnp.float32) + h
            block = step * 128 + tile * GROUPS * 2 + 2 * i
            valid = jnp.concatenate([sub16 < counts_ref[block], sub16 < counts_ref[block + 1]], 0)
            value = jnp.where(valid, jnp.maximum(h, 0.0), 0.0).astype(jnp.bfloat16)
            out_ref[pl.ds(row, 16), :] = value
            if second:
                fine_ref[pl.ds(row, 16), :] = value.astype(jnp.float32)
        return 0

    lax.fori_loop(0, 8, epilogue, 0)

    if second:

        @pl.when(step == 3)
        def _():

            def down(c, _):
                total = jnp.zeros((64, 256), jnp.float32)
                for j in range(8):
                    child = fine_ref[pl.ds(c * 512 + j, 64, stride=8), :].astype(jnp.bfloat16)
                    total += jnp.dot(child, wd_ref[j * 128 : (j + 1) * 128, :], preferred_element_type=jnp.float32)
                value = jnp.maximum(normed(total, gain_down_ref[...]), 0.0)
                row = pl.multiple_of(c * 64, 64)
                raw[pl.ds(row, 64), :] = value[:, :128]
                raw[pl.ds(row + 512, 64), :] = value[:, 128:]
                return 0

            lax.fori_loop(0, 8, down, 0)
            for n, row in enumerate((0, 448)):
                for h in range(2):
                    edge_ref[n * 64 : n * 64 + 64, h * 128 : h * 128 + 128] = raw[
                        h * 512 + row : h * 512 + row + 64, :
                    ].astype(jnp.bfloat16)
            placed[...] = jnp.zeros_like(placed)

            def put(g, _):
                for i in range(16):
                    at = place_ref[g * 16 + i]
                    placed[pl.ds(at, 1), :] = raw[pl.ds(g * 16 + i, 1), :]
                    placed[pl.ds(at + 520, 1), :] = raw[pl.ds(g * 16 + i + 512, 1), :]
                return 0

            lax.fori_loop(0, 32, put, 0)
            down_ref[:, :128] = placed[:512, :].astype(jnp.bfloat16)
            down_ref[:, 128:] = placed[520:1032, :].astype(jnp.bfloat16)


def whole(shape):
    return pl.BlockSpec(shape, lambda i: (0,) * len(shape))


def conv(second, idx, plan, counts, lo, mid, hi, w, gain, *more, places=()):
    specs = [
        pl.BlockSpec((8 * K * TILE,), lambda i: (i,), memory_space=pltpu.SMEM),
        pl.BlockSpec(memory_space=pltpu.SMEM),
        pl.BlockSpec(memory_space=pltpu.SMEM),
    ] + [whole(a.shape) for a in (lo, mid, hi, w, gain) + more]
    specs += [pl.BlockSpec(memory_space=pltpu.SMEM) for _ in places]
    out_shape = [jax.ShapeDtypeStruct((4096, 128), jnp.bfloat16)]
    scratch = [
        pltpu.VMEM((PAD + 6144 + 8, 128), jnp.float32),
        pltpu.VMEM((1024, len(OTHERS) * 128), jnp.bfloat16),
        pltpu.VMEM((1024 + 8, 128), jnp.float32),
        pltpu.VMEM((len(OTHERS) * 128, 128), jnp.bfloat16),
        pltpu.VMEM((1024, 128), jnp.float32),
    ]
    if second:
        out_shape.append(jax.ShapeDtypeStruct((512, 256), jnp.bfloat16))
        out_shape.append(jax.ShapeDtypeStruct((128, 256), jnp.bfloat16))
        scratch.append(pltpu.VMEM((4096, 128), jnp.float32))
        scratch.append(pltpu.VMEM((1024, 128), jnp.float32))
        scratch.append(pltpu.VMEM((1040, 128), jnp.float32))
    return pl.pallas_call(
        functools.partial(conv_kernel, second),
        grid=(4,),
        in_specs=specs,
        out_specs=[whole(s.shape) for s in out_shape],
        out_shape=out_shape,
        scratch_shapes=scratch,
        name="conv_second" if second else "conv_first",
        compiler_params=pltpu.CompilerParams(vmem_limit_bytes=VMEM_LIMIT),
    )(idx, plan, counts, lo, mid, hi, w, gain, *more, *places)


HALF = 2048 + 16
NOWHERE = PAD + 2048
REACH = 640


def ring(axis):
    me, count = lax.axis_index(axis), lax.axis_size(axis)
    return lax.rem(me + 1, count), lax.rem(me + count - 1, count)


def greet(partners):
    barrier = pltpu.get_barrier_semaphore()
    for partner in partners:
        pl.semaphore_signal(barrier, inc=1, device_id=partner, device_id_type=pl.DeviceIdType.MESH)
    pl.semaphore_wait(barrier, len(partners))


def sender(send_sem, recv_sem):
    count = [0]

    def send(src, dst, partner):
        n = count[0]
        count[0] += 1
        copy = pltpu.make_async_remote_copy(
            src_ref=src,
            dst_ref=dst,
            send_sem=send_sem.at[n],
            recv_sem=recv_sem.at[n],
            device_id=partner,
            device_id_type=pl.DeviceIdType.MESH,
        )
        copy.start()
        return copy

    return send


def halo_kernel(field_ref, lo_ref, hi_ref, send_sem, recv_sem):
    tile = lax.axis_index("tile")
    above, below = ring("morton")
    greet([(tile, above), (tile, below)])
    send = sender(send_sem, recv_sem)
    copies = [
        send(field_ref.at[pl.ds(3072, 1024)], lo_ref, (tile, above)),
        send(field_ref.at[pl.ds(0, 1024)], hi_ref, (tile, below)),
    ]
    for copy in copies:
        copy.wait()


def halo_of(field):
    return pl.pallas_call(
        halo_kernel,
        in_specs=[pl.BlockSpec(memory_space=pl.ANY)],
        out_specs=[pl.BlockSpec(memory_space=pl.ANY)] * 2,
        out_shape=[jax.ShapeDtypeStruct((1024, 128), jnp.bfloat16)] * 2,
        scratch_shapes=[pltpu.SemaphoreType.DMA((2,)), pltpu.SemaphoreType.DMA((2,))],
        name="halo",
        compiler_params=pltpu.CompilerParams(collective_id=1, has_side_effects=True),
    )(field)


def exchange_kernel(rows_ref, edge_ref, codes_ref, pool_ref, places_ref, send_sem, recv_sem, local_sem):
    tile, me = lax.axis_index("tile"), lax.axis_index("morton")
    right, left = ring("tile")
    above, below = ring("morton")
    opposite = lax.rem(tile + 2, lax.axis_size("tile"))
    tiles = (tile, right, left, opposite)
    greet([(right, me), (left, me)] + [(t, m) for t in tiles for m in (above, below)])

    send = sender(send_sem, recv_sem)
    first, last = pl.ds(0, 256), pl.ds(256, 256)
    from_below, from_above = pl.ds(512, 64), pl.ds(576, 64)
    right_first = send(rows_ref.at[first], pool_ref.at[tile, first], (right, me))
    left_last = send(rows_ref.at[last], pool_ref.at[tile, last], (left, me))
    handed = {}
    for n, t in enumerate((right, left, tile)):
        handed[n, 0] = send(edge_ref.at[pl.ds(64, 64)], pool_ref.at[tile, from_below], (t, above))
        handed[n, 1] = send(edge_ref.at[pl.ds(0, 64)], pool_ref.at[tile, from_above], (t, below))
    others = [send(rows_ref.at[last], pool_ref.at[tile, last], (right, me))]
    others.append(send(rows_ref.at[first], pool_ref.at[tile, first], (left, me)))
    for t in tiles:
        others.append(send(codes_ref, places_ref.at[0, tile], (t, above)))
        others.append(send(codes_ref, places_ref.at[1, tile], (t, below)))
    own = pltpu.make_async_copy(rows_ref, pool_ref.at[tile, pl.ds(0, 512)], local_sem)
    own.start()

    relays = ((right_first, left, first, right), (left_last, right, last, left))
    relays += ((handed[0, 0], left, from_below, right), (handed[1, 1], right, from_above, left))
    passed = []
    for copy, source, part, target in relays:
        copy.wait_recv()
        passed.append(send(pool_ref.at[source, part], pool_ref.at[source, part], (target, me)))
    for copy, _, _, _ in relays:
        copy.wait_send()
    own.wait()
    for copy in [handed[0, 1], handed[1, 0], handed[2, 0], handed[2, 1]] + others + passed:
        copy.wait()


def exchange(rows, edges, codes):
    return pl.pallas_call(
        exchange_kernel,
        in_specs=[pl.BlockSpec(memory_space=pl.ANY)] * 3,
        out_specs=[pl.BlockSpec(memory_space=pl.ANY)] * 2,
        out_shape=[
            jax.ShapeDtypeStruct((4, REACH, 256), jnp.bfloat16),
            jax.ShapeDtypeStruct((2, 4, 8, 128), jnp.int32),
        ],
        scratch_shapes=[
            pltpu.SemaphoreType.DMA((22,)),
            pltpu.SemaphoreType.DMA((22,)),
            pltpu.SemaphoreType.DMA,
        ],
        name="exchange",
        compiler_params=pltpu.CompilerParams(collective_id=0, has_side_effects=True),
    )(rows, edges, codes)


def coarse_kernel(idx_ref, places_ref, pool_ref, w_in, gain_ref, out_ref, table, source, gathered, acc_ref):
    masks = sublane_masks()
    table[:PAD, :] = jnp.zeros((PAD, 128), jnp.float32)
    table[HALF : HALF + PAD, :] = jnp.zeros((PAD, 128), jnp.float32)

    def tile_rows(t, _):
        row = pl.multiple_of(PAD + t * 512, 8)
        for h in range(2):
            cols = slice(h * 128, h * 128 + 128)
            table[pl.ds(row + h * HALF, 512), :] = pool_ref[t, :512, cols].astype(jnp.float32)
            source[pl.ds((t * 2 + h) * 128, 128), :] = pool_ref[t, 512:, cols].astype(jnp.float32)
        return 0

    lax.fori_loop(0, 4, tile_rows, 0)

    def handed(t, _):
        for kind in range(2):
            for i in range(64):
                at = places_ref[kind, t, 0, kind * 64 + i]
                row = t * 256 + kind * 64 + i
                table[pl.ds(at, 1), :] = source[pl.ds(row, 1), :]
                table[pl.ds(at + HALF, 1), :] = source[pl.ds(row + 128, 1), :]
        return 0

    lax.fori_loop(0, 4, handed, 0)
    gather_rows(idx_ref, ((table, 0), (table, HALF)), gathered, 4, masks)
    acc_ref[...] = jnp.dot(gathered[...], w_in[...], preferred_element_type=jnp.float32)
    first = PAD + 512 * lax.axis_index("tile")

    def epilogue(tile, _):
        for i in range(GROUPS):
            row = pl.multiple_of(tile * TILE + i * 16, 16)
            h = normed(acc_ref[pl.ds(row, 16), :], gain_ref[...])
            at = pl.multiple_of(first + row, 8)
            own = jnp.concatenate([table[pl.ds(at, 16), :], table[pl.ds(at + HALF, 16), :]], 1)
            out_ref[pl.ds(row, 16), :] = jnp.maximum(own + h, 0.0).astype(jnp.bfloat16)
        return 0

    lax.fori_loop(0, 4, epilogue, 0)


def coarse(idx, places, pool, w, gain):
    return pl.pallas_call(
        coarse_kernel,
        in_specs=[pl.BlockSpec(memory_space=pltpu.SMEM)] * 2 + [pl.BlockSpec(memory_space=pltpu.VMEM)] * 3,
        out_specs=pl.BlockSpec(memory_space=pltpu.VMEM),
        out_shape=jax.ShapeDtypeStruct((512, 256), jnp.bfloat16),
        scratch_shapes=[
            pltpu.VMEM((2 * HALF, 128), jnp.float32),
            pltpu.VMEM((1024, 128), jnp.float32),
            pltpu.VMEM((512, K * 256), jnp.bfloat16),
            pltpu.VMEM((512, 256), jnp.float32),
        ],
        name="coarse",
        compiler_params=pltpu.CompilerParams(vmem_limit_bytes=VMEM_LIMIT),
    )(idx, places, pool, w, gain)


def by_tiles(index):
    return index.reshape(K, -1, 1, TILE).transpose(1, 0, 2, 3).reshape(-1)


def plan_of(counts):
    held = counts.reshape(4, 128)
    block = jnp.arange(128, dtype=jnp.int32)
    ends = jnp.sum(jnp.where(block[None, :] <= block[:, None], held[:, None, :], 0), axis=-1)
    place = jnp.arange(LISTED, dtype=jnp.int32)
    past = ends[:, None, :] <= place[None, :, None]
    at = jnp.sum(past.astype(jnp.int32), axis=-1)
    start = jnp.max(jnp.where(past, ends[:, None, :], 0), axis=-1)
    entry = (at // 16) * (K * TILE) + (at % 16) * 8 + place[None, :] - start
    listed = jnp.where(at < 128, entry, 0)
    rest = jnp.broadcast_to(ends[:, 127:], (4, PLAN - LISTED - 128))
    return jnp.concatenate([listed, ends - held, rest], axis=1).reshape(-1)


def shards(
    features,
    neighbours,
    counts,
    owner,
    slot,
    coarse_neighbours,
    w_first,
    w_second,
    w_down,
    w_coarse,
    gain_first,
    gain_second,
    gain_down,
    gain_coarse,
):
    lane_ids = jnp.arange(8, dtype=jnp.int32)

    def masked(first):
        valid = lane_ids[None, :] < counts[0, first : first + 128, None]
        rows = features[0, 8 * first : 8 * first + 1024].reshape(128, 8, 128)
        return jnp.where(valid[:, :, None], rows, 0).astype(jnp.bfloat16).reshape(1024, 128)

    lo, hi = shifted(masked(384), "morton", 1), shifted(masked(0), "morton", -1)
    by_offset = neighbours[0].T
    local = by_offset + jnp.arange(4096, dtype=jnp.int32)[None, :]
    idx = by_tiles(jnp.where(by_offset < 0, -1, local))
    plan = plan_of(counts[0])
    coarse_idx = by_tiles(coarse_neighbours[0].T)

    me = lax.axis_index("morton")
    destination = owner[0]
    at = PAD + 512 * lax.axis_index("tile") + slot[0]

    def handed(to):
        return jnp.where(destination == to, at, NOWHERE)

    edges = jnp.concatenate([handed(me + 1)[448:], handed(me - 1)[:64]])
    codes = jnp.broadcast_to(edges[None], (8, 128))
    kept = jnp.where(destination == me, slot[0], 512)

    (act,) = conv(False, idx, plan, counts[0], lo, features[0], hi, w_first, gain_first[None])
    lo, hi = halo_of(act)
    fine, rows, edge_rows = conv(
        True, idx, plan, counts[0], lo, act, hi, w_second, gain_second[None], features[0], w_down, gain_down[None], places=(kept,)
    )
    pool, places = exchange(rows, edge_rows, codes)
    out = coarse(coarse_idx, places, pool, w_coarse, gain_coarse[None])
    return fine[None], out[None]


def solution(mesh):
    split = P("tile", "morton", None)
    flat = P("tile", "morton")
    in_specs = (split, split, flat, flat, flat, split) + (P(),) * 8
    return jax.shard_map(shards, mesh=mesh, in_specs=in_specs, out_specs=(split, split), check_vma=False)
```

```python
import functools

import jax
import jax.numpy as jnp
from jax import lax
from jax.experimental import pallas as pl
from jax.experimental.pallas import tpu as pltpu
from jax.sharding import PartitionSpec as P

K = 27
SELF = 13
OTHERS = tuple(k for k in range(K) if k != SELF)
TILE = 128
GROUPS = TILE // 16
PAD = 8
PLAN = 1280
LISTED = 1056
MOSTLY = 640
EPS = 1e-05
VMEM_LIMIT = 34 * 2**20


def shifted(value, axis, steps):
    count = lax.axis_size(axis)
    initial, last = (max(0, -steps), min(count, count - steps))
    return lax.ppermute(value, axis, [(source, source + steps) for source in range(initial, last)])


def sublane_masks():
    sub = lax.broadcasted_iota(jnp.int32, (8, 128), 0)
    return [sub == i for i in range(8)]


def gather_rows(idx_ref, tables, dst_ref, tiles, masks):
    width = 128 * len(tables)

    def body(step, _):
        for part in range(2):
            g = step * 2 + part
            base_ref = idx_ref.at[pl.ds((step // 4) * (K * TILE) + (step % 4) * 32, (K - 1) * TILE + 32)]
            for k in range(K):
                both = [[] for _ in tables]
                for h in range(2):
                    first = k * TILE + part * 16 + h * 8
                    lead = 8 if first else 0
                    at = base_ref.at[pl.ds(first - lead, 8 + lead)]
                    acc = [None for _ in tables]
                    for i in range(8):
                        row = at[lead + i]
                        for n, (table, base) in enumerate(tables):
                            v = table[pl.ds(row + (base + PAD - i), 8), :]
                            acc[n] = v if i == 0 else jnp.where(masks[i], v, acc[n])
                    for n in range(len(tables)):
                        both[n].append(acc[n])
                for n in range(len(tables)):
                    col = k * width + n * 128
                    dst_ref[pl.ds(pl.multiple_of(g * 16, 16), 16), col : col + 128] = jnp.concatenate(
                        both[n], 0
                    ).astype(jnp.bfloat16)
        return 0

    lax.fori_loop(0, tiles * 4, body, 0)


def gather_listed(idx_ref, plan_ref, first, groups, table, dst_ref, masks):
    def body(g, _):
        both = []
        for h in range(2):
            listed = plan_ref.at[pl.ds(first + g * 16 + h * 8, 8)]
            at = [idx_ref.at[pl.ds(listed[i], (K - 1) * TILE + 1)] for i in range(8)]
            both.append([])
            for n, k in enumerate(OTHERS):
                acc = None
                for i in range(8):
                    v = table[pl.ds(at[i][k * TILE] + (PAD - i), 8), :]
                    acc = v if i == 0 else jnp.where(masks[i], v, acc)
                both[h].append(acc)
                if h:
                    dst_ref[pl.ds(pl.multiple_of(g * 16, 16), 16), n * 128 : n * 128 + 128] = jnp.concatenate(
                        [both[0][n], acc], 0
                    ).astype(jnp.bfloat16)
        return 0

    lax.fori_loop(0, groups, body, 0)


def normed(h, gain):
    return h * lax.rsqrt(jnp.mean(h * h, axis=-1, keepdims=True) + EPS) * gain


def conv_kernel(
    second,
    idx_ref,
    plan_ref,
    counts_ref,
    lo_ref,
    mid_ref,
    hi_ref,
    w_in,
    gain_ref,
    *rest,
):
    if second:
        x_ref, wd_ref, gain_down_ref, place_ref, out_ref, down_ref, edge_ref, table, gathered, acc_ref, w_ref, self_ref, fine_ref, raw, placed = rest
    else:
        out_ref, table, gathered, acc_ref, w_ref, self_ref = rest
    step = pl.program_id(0)
    masks = sublane_masks()
    sub16 = lax.broadcasted_iota(jnp.int32, (8, 128), 0)

    @pl.when(step == 0)
    def _():
        table[:PAD, :] = jnp.zeros((PAD, 128), jnp.float32)
        w_ref[: SELF * 128, :] = w_in[: SELF * 128, :]
        w_ref[SELF * 128 :, :] = w_in[(SELF + 1) * 128 :, :]
        table[pl.ds(PAD, 1024), :] = lo_ref[...].astype(jnp.float32)
        if second:
            table[pl.ds(PAD + 1024, 4096), :] = mid_ref[...].astype(jnp.float32)
        else:

            def masked(g, _):
                for i in range(8):
                    block = g * 16 + 2 * i
                    row = pl.multiple_of(block * 8, 16)
                    valid = jnp.concatenate([sub16 < counts_ref[block], sub16 < counts_ref[block + 1]], 0)
                    value = jnp.where(valid, mid_ref[pl.ds(row, 16), :].astype(jnp.float32), 0.0)
                    table[pl.ds(pl.multiple_of(row + (PAD + 1024), 8), 16), :] = value
                return 0

            lax.fori_loop(0, 32, masked, 0)
        table[pl.ds(PAD + 5120, 1024), :] = hi_ref[...].astype(jnp.float32)

    plan = step * PLAN
    total = plan_ref[plan + LISTED + 128]
    gather_listed(idx_ref, plan_ref, plan, (total + 15) // 16, table, gathered, masks)
    own = mid_ref[pl.ds(pl.multiple_of(step * 1024, 1024), 1024), :]
    self_ref[...] = jnp.dot(own, w_in[SELF * 128 : (SELF + 1) * 128, :], preferred_element_type=jnp.float32)
    acc_ref[:MOSTLY, :] = jnp.dot(gathered[:MOSTLY, :], w_ref[...], preferred_element_type=jnp.float32)

    @pl.when(total > MOSTLY)
    def _():
        acc_ref[MOSTLY:1024, :] = jnp.dot(gathered[MOSTLY:, :], w_ref[...], preferred_element_type=jnp.float32)

    def epilogue(tile, _):
        gain = gain_ref[...]
        for i in range(GROUPS):
            start = plan_ref.at[pl.ds(plan + LISTED + tile * GROUPS * 2 + 2 * i, 2)]
            h = jnp.concatenate([acc_ref[pl.ds(start[0], 8), :], acc_ref[pl.ds(start[1], 8), :]], 0)
            h = normed(h + self_ref[pl.ds(pl.multiple_of(tile * TILE + i * 16, 16), 16), :], gain)
            row = pl.multiple_of(step * 1024 + tile * TILE + i * 16, 16)
            if second:
                h = x_ref[pl.ds(row, 16), :].astype(jnp.float32) + h
            block = step * 128 + tile * GROUPS * 2 + 2 * i
            valid = jnp.concatenate([sub16 < counts_ref[block], sub16 < counts_ref[block + 1]], 0)
            value = jnp.where(valid, jnp.maximum(h, 0.0), 0.0).astype(jnp.bfloat16)
            out_ref[pl.ds(row, 16), :] = value
            if second:
                fine_ref[pl.ds(row, 16), :] = value.astype(jnp.float32)
        return 0

    lax.fori_loop(0, 8, epilogue, 0)

    if second:

        @pl.when(step == 3)
        def _():

            def down(c, _):
                total = jnp.zeros((64, 256), jnp.float32)
                for j in range(8):
                    child = fine_ref[pl.ds(c * 512 + j, 64, stride=8), :].astype(jnp.bfloat16)
                    total += jnp.dot(child, wd_ref[j * 128 : (j + 1) * 128, :], preferred_element_type=jnp.float32)
                value = jnp.maximum(normed(total, gain_down_ref[...]), 0.0)
                row = pl.multiple_of(c * 64, 64)
                raw[pl.ds(row, 64), :] = value[:, :128]
                raw[pl.ds(row + 512, 64), :] = value[:, 128:]
                return 0

            lax.fori_loop(0, 8, down, 0)
            for n, row in enumerate((0, 448)):
                for h in range(2):
                    edge_ref[n * 64 : n * 64 + 64, h * 128 : h * 128 + 128] = raw[
                        h * 512 + row : h * 512 + row + 64, :
                    ].astype(jnp.bfloat16)
            placed[...] = jnp.zeros_like(placed)

            def put(g, _):
                for i in range(16):
                    at = place_ref[g * 16 + i]
                    placed[pl.ds(at, 1), :] = raw[pl.ds(g * 16 + i, 1), :]
                    placed[pl.ds(at + 520, 1), :] = raw[pl.ds(g * 16 + i + 512, 1), :]
                return 0

            lax.fori_loop(0, 32, put, 0)
            down_ref[:, :128] = placed[:512, :].astype(jnp.bfloat16)
            down_ref[:, 128:] = placed[520:1032, :].astype(jnp.bfloat16)


def whole(shape):
    return pl.BlockSpec(shape, lambda i: (0,) * len(shape))


def conv(second, idx, plan, counts, lo, mid, hi, w, gain, *more, places=()):
    specs = [
        pl.BlockSpec((8 * K * TILE,), lambda i: (i,), memory_space=pltpu.SMEM),
        pl.BlockSpec(memory_space=pltpu.SMEM),
        pl.BlockSpec(memory_space=pltpu.SMEM),
    ] + [whole(a.shape) for a in (lo, mid, hi, w, gain) + more]
    specs += [pl.BlockSpec(memory_space=pltpu.SMEM) for _ in places]
    out_shape = [jax.ShapeDtypeStruct((4096, 128), jnp.bfloat16)]
    scratch = [
        pltpu.VMEM((PAD + 6144 + 8, 128), jnp.float32),
        pltpu.VMEM((1024, len(OTHERS) * 128), jnp.bfloat16),
        pltpu.VMEM((1024 + 8, 128), jnp.float32),
        pltpu.VMEM((len(OTHERS) * 128, 128), jnp.bfloat16),
        pltpu.VMEM((1024, 128), jnp.float32),
    ]
    if second:
        out_shape.append(jax.ShapeDtypeStruct((512, 256), jnp.bfloat16))
        out_shape.append(jax.ShapeDtypeStruct((128, 256), jnp.bfloat16))
        scratch.append(pltpu.VMEM((4096, 128), jnp.float32))
        scratch.append(pltpu.VMEM((1024, 128), jnp.float32))
        scratch.append(pltpu.VMEM((1040, 128), jnp.float32))
    return pl.pallas_call(
        functools.partial(conv_kernel, second),
        grid=(4,),
        in_specs=specs,
        out_specs=[whole(s.shape) for s in out_shape],
        out_shape=out_shape,
        scratch_shapes=scratch,
        name="conv_second" if second else "conv_first",
        compiler_params=pltpu.CompilerParams(vmem_limit_bytes=VMEM_LIMIT),
    )(idx, plan, counts, lo, mid, hi, w, gain, *more, *places)


HALF = 2048 + 16
NOWHERE = PAD + 2048
REACH = 640


def ring(axis):
    me, count = lax.axis_index(axis), lax.axis_size(axis)
    return lax.rem(me + 1, count), lax.rem(me + count - 1, count)


def greet(partners):
    barrier = pltpu.get_barrier_semaphore()
    for partner in partners:
        pl.semaphore_signal(barrier, inc=1, device_id=partner, device_id_type=pl.DeviceIdType.MESH)
    pl.semaphore_wait(barrier, len(partners))


def sender(send_sem, recv_sem):
    count = [0]

    def send(src, dst, partner):
        n = count[0]
        count[0] += 1
        copy = pltpu.make_async_remote_copy(
            src_ref=src,
            dst_ref=dst,
            send_sem=send_sem.at[n],
            recv_sem=recv_sem.at[n],
            device_id=partner,
            device_id_type=pl.DeviceIdType.MESH,
        )
        copy.start()
        return copy

    return send


def halo_kernel(field_ref, lo_ref, hi_ref, send_sem, recv_sem):
    tile = lax.axis_index("tile")
    above, below = ring("morton")
    greet([(tile, above), (tile, below)])
    send = sender(send_sem, recv_sem)
    copies = [
        send(field_ref.at[pl.ds(3072, 1024)], lo_ref, (tile, above)),
        send(field_ref.at[pl.ds(0, 1024)], hi_ref, (tile, below)),
    ]
    for copy in copies:
        copy.wait()


def halo_of(field):
    return pl.pallas_call(
        halo_kernel,
        in_specs=[pl.BlockSpec(memory_space=pl.ANY)],
        out_specs=[pl.BlockSpec(memory_space=pl.ANY)] * 2,
        out_shape=[jax.ShapeDtypeStruct((1024, 128), jnp.bfloat16)] * 2,
        scratch_shapes=[pltpu.SemaphoreType.DMA((2,)), pltpu.SemaphoreType.DMA((2,))],
        name="halo",
        compiler_params=pltpu.CompilerParams(collective_id=1, has_side_effects=True),
    )(field)


def exchange_kernel(rows_ref, edge_ref, codes_ref, pool_ref, places_ref, send_sem, recv_sem, local_sem):
    tile, me = lax.axis_index("tile"), lax.axis_index("morton")
    right, left = ring("tile")
    above, below = ring("morton")
    opposite = lax.rem(tile + 2, lax.axis_size("tile"))
    tiles = (tile, right, left, opposite)
    greet([(right, me), (left, me)] + [(t, m) for t in tiles for m in (above, below)])

    send = sender(send_sem, recv_sem)
    first, last = pl.ds(0, 256), pl.ds(256, 256)
    from_below, from_above = pl.ds(512, 64), pl.ds(576, 64)
    right_first = send(rows_ref.at[first], pool_ref.at[tile, first], (right, me))
    left_last = send(rows_ref.at[last], pool_ref.at[tile, last], (left, me))
    handed = {}
    for n, t in enumerate((right, left, tile)):
        handed[n, 0] = send(edge_ref.at[pl.ds(64, 64)], pool_ref.at[tile, from_below], (t, above))
        handed[n, 1] = send(edge_ref.at[pl.ds(0, 64)], pool_ref.at[tile, from_above], (t, below))
    others = [send(rows_ref.at[last], pool_ref.at[tile, last], (right, me))]
    others.append(send(rows_ref.at[first], pool_ref.at[tile, first], (left, me)))
    for t in tiles:
        others.append(send(codes_ref, places_ref.at[0, tile], (t, above)))
        others.append(send(codes_ref, places_ref.at[1, tile], (t, below)))
    own = pltpu.make_async_copy(rows_ref, pool_ref.at[tile, pl.ds(0, 512)], local_sem)
    own.start()

    relays = ((right_first, left, first, right), (left_last, right, last, left))
    relays += ((handed[0, 0], left, from_below, right), (handed[1, 1], right, from_above, left))
    passed = []
    for copy, source, part, target in relays:
        copy.wait_recv()
        passed.append(send(pool_ref.at[source, part], pool_ref.at[source, part], (target, me)))
    for copy, _, _, _ in relays:
        copy.wait_send()
    own.wait()
    for copy in [handed[0, 1], handed[1, 0], handed[2, 0], handed[2, 1]] + others + passed:
        copy.wait()


def exchange(rows, edges, codes):
    return pl.pallas_call(
        exchange_kernel,
        in_specs=[pl.BlockSpec(memory_space=pl.ANY)] * 3,
        out_specs=[pl.BlockSpec(memory_space=pl.ANY)] * 2,
        out_shape=[
            jax.ShapeDtypeStruct((4, REACH, 256), jnp.bfloat16),
            jax.ShapeDtypeStruct((2, 4, 8, 128), jnp.int32),
        ],
        scratch_shapes=[
            pltpu.SemaphoreType.DMA((22,)),
            pltpu.SemaphoreType.DMA((22,)),
            pltpu.SemaphoreType.DMA,
        ],
        name="exchange",
        compiler_params=pltpu.CompilerParams(collective_id=0, has_side_effects=True),
    )(rows, edges, codes)


def coarse_kernel(idx_ref, places_ref, pool_ref, w_in, gain_ref, out_ref, table, source, gathered, acc_ref):
    masks = sublane_masks()
    table[:PAD, :] = jnp.zeros((PAD, 128), jnp.float32)
    table[HALF : HALF + PAD, :] = jnp.zeros((PAD, 128), jnp.float32)

    def tile_rows(t, _):
        row = pl.multiple_of(PAD + t * 512, 8)
        for h in range(2):
            cols = slice(h * 128, h * 128 + 128)
            table[pl.ds(row + h * HALF, 512), :] = pool_ref[t, :512, cols].astype(jnp.float32)
            source[pl.ds((t * 2 + h) * 128, 128), :] = pool_ref[t, 512:, cols].astype(jnp.float32)
        return 0

    lax.fori_loop(0, 4, tile_rows, 0)

    def handed(t, _):
        for kind in range(2):
            for i in range(64):
                at = places_ref[kind, t, 0, kind * 64 + i]
                row = t * 256 + kind * 64 + i
                table[pl.ds(at, 1), :] = source[pl.ds(row, 1), :]
                table[pl.ds(at + HALF, 1), :] = source[pl.ds(row + 128, 1), :]
        return 0

    lax.fori_loop(0, 4, handed, 0)
    gather_rows(idx_ref, ((table, 0), (table, HALF)), gathered, 4, masks)
    acc_ref[...] = jnp.dot(gathered[...], w_in[...], preferred_element_type=jnp.float32)
    first = PAD + 512 * lax.axis_index("tile")

    def epilogue(tile, _):
        for i in range(GROUPS):
            row = pl.multiple_of(tile * TILE + i * 16, 16)
            h = normed(acc_ref[pl.ds(row, 16), :], gain_ref[...])
            at = pl.multiple_of(first + row, 8)
            own = jnp.concatenate([table[pl.ds(at, 16), :], table[pl.ds(at + HALF, 16), :]], 1)
            out_ref[pl.ds(row, 16), :] = jnp.maximum(own + h, 0.0).astype(jnp.bfloat16)
        return 0

    lax.fori_loop(0, 4, epilogue, 0)


def coarse(idx, places, pool, w, gain):
    return pl.pallas_call(
        coarse_kernel,
        in_specs=[pl.BlockSpec(memory_space=pltpu.SMEM)] * 2 + [pl.BlockSpec(memory_space=pltpu.VMEM)] * 3,
        out_specs=pl.BlockSpec(memory_space=pltpu.VMEM),
        out_shape=jax.ShapeDtypeStruct((512, 256), jnp.bfloat16),
        scratch_shapes=[
            pltpu.VMEM((2 * HALF, 128), jnp.float32),
            pltpu.VMEM((1024, 128), jnp.float32),
            pltpu.VMEM((512, K * 256), jnp.bfloat16),
            pltpu.VMEM((512, 256), jnp.float32),
        ],
        name="coarse",
        compiler_params=pltpu.CompilerParams(vmem_limit_bytes=VMEM_LIMIT),
    )(idx, places, pool, w, gain)


def by_tiles(index):
    return index.reshape(K, -1, 1, TILE).transpose(1, 0, 2, 3).reshape(-1)


def plan_of(counts):
    held = counts.reshape(4, 128)
    block = jnp.arange(128, dtype=jnp.int32)
    ends = jnp.sum(jnp.where(block[None, :] <= block[:, None], held[:, None, :], 0), axis=-1)
    place = jnp.arange(LISTED, dtype=jnp.int32)
    past = ends[:, None, :] <= place[None, :, None]
    at = jnp.sum(past.astype(jnp.int32), axis=-1)
    start = jnp.max(jnp.where(past, ends[:, None, :], 0), axis=-1)
    entry = (at // 16) * (K * TILE) + (at % 16) * 8 + place[None, :] - start
    listed = jnp.where(at < 128, entry, 0)
    rest = jnp.broadcast_to(ends[:, 127:], (4, PLAN - LISTED - 128))
    return jnp.concatenate([listed, ends - held, rest], axis=1).reshape(-1)


def shards(
    features,
    neighbours,
    counts,
    owner,
    slot,
    coarse_neighbours,
    w_first,
    w_second,
    w_down,
    w_coarse,
    gain_first,
    gain_second,
    gain_down,
    gain_coarse,
):
    lane_ids = jnp.arange(8, dtype=jnp.int32)

    def masked(first):
        valid = lane_ids[None, :] < counts[0, first : first + 128, None]
        rows = features[0, 8 * first : 8 * first + 1024].reshape(128, 8, 128)
        return jnp.where(valid[:, :, None], rows, 0).astype(jnp.bfloat16).reshape(1024, 128)

    lo, hi = shifted(masked(384), "morton", 1), shifted(masked(0), "morton", -1)
    by_offset = neighbours[0].T
    local = by_offset + jnp.arange(4096, dtype=jnp.int32)[None, :]
    idx = by_tiles(jnp.where(by_offset < 0, -1, local))
    plan = plan_of(counts[0])
    coarse_idx = by_tiles(coarse_neighbours[0].T)

    me = lax.axis_index("morton")
    destination = owner[0]
    at = PAD + 512 * lax.axis_index("tile") + slot[0]

    def handed(to):
        return jnp.where(destination == to, at, NOWHERE)

    edges = jnp.concatenate([handed(me + 1)[448:], handed(me - 1)[:64]])
    codes = jnp.broadcast_to(edges[None], (8, 128))
    kept = jnp.where(destination == me, slot[0], 512)

    (act,) = conv(False, idx, plan, counts[0], lo, features[0], hi, w_first, gain_first[None])
    lo, hi = halo_of(act)
    fine, rows, edge_rows = conv(
        True, idx, plan, counts[0], lo, act, hi, w_second, gain_second[None], features[0], w_down, gain_down[None], places=(kept,)
    )
    pool, places = exchange(rows, edge_rows, codes)
    out = coarse(coarse_idx, places, pool, w_coarse, gain_coarse[None])
    return fine[None], out[None]


def solution(mesh):
    split = P("tile", "morton", None)
    flat = P("tile", "morton")
    in_specs = (split, split, flat, flat, flat, split) + (P(),) * 8
    return jax.shard_map(shards, mesh=mesh, in_specs=in_specs, out_specs=(split, split), check_vma=False)
```

```python
import functools

import jax
import jax.numpy as jnp
from jax import lax
from jax.experimental import pallas as pl
from jax.experimental.pallas import tpu as pltpu
from jax.sharding import PartitionSpec as P

K = 27
SELF = 13
OTHERS = tuple(k for k in range(K) if k != SELF)
TILE = 128
GROUPS = TILE // 16
PAD = 8
PLAN = 1280
LISTED = 1056
MOSTLY = 640
EPS = 1e-05
VMEM_LIMIT = 58 * 2**20


def shifted(value, axis, steps):
    count = lax.axis_size(axis)
    initial, last = (max(0, -steps), min(count, count - steps))
    return lax.ppermute(value, axis, [(source, source + steps) for source in range(initial, last)])


def sublane_masks():
    sub = lax.broadcasted_iota(jnp.int32, (8, 128), 0)
    return [sub == i for i in range(8)]


def gather_rows(idx_ref, tables, dst_ref, tiles, masks):
    width = 128 * len(tables)

    def body(step, _):
        for part in range(2):
            g = step * 2 + part
            base_ref = idx_ref.at[pl.ds((step // 4) * (K * TILE) + (step % 4) * 32, (K - 1) * TILE + 32)]
            for k in range(K):
                both = [[] for _ in tables]
                for h in range(2):
                    first = k * TILE + part * 16 + h * 8
                    lead = 8 if first else 0
                    at = base_ref.at[pl.ds(first - lead, 8 + lead)]
                    acc = [None for _ in tables]
                    for i in range(8):
                        row = at[lead + i]
                        for n, (table, base) in enumerate(tables):
                            v = table[pl.ds(row + (base + PAD - i), 8), :]
                            acc[n] = v if i == 0 else jnp.where(masks[i], v, acc[n])
                    for n in range(len(tables)):
                        both[n].append(acc[n])
                for n in range(len(tables)):
                    col = k * width + n * 128
                    dst_ref[pl.ds(pl.multiple_of(g * 16, 16), 16), col : col + 128] = jnp.concatenate(
                        both[n], 0
                    ).astype(jnp.bfloat16)
        return 0

    lax.fori_loop(0, tiles * 4, body, 0)


def gather_listed(idx_ref, plan_ref, first, groups, table, dst_ref, masks):
    def body(g, _):
        both = []
        for h in range(2):
            listed = plan_ref.at[pl.ds(first + g * 16 + h * 8, 8)]
            at = [idx_ref.at[pl.ds(listed[i], (K - 1) * TILE + 1)] for i in range(8)]
            both.append([])
            for n, k in enumerate(OTHERS):
                acc = None
                for i in range(8):
                    v = table[pl.ds(at[i][k * TILE] + (PAD - i), 8), :]
                    acc = v if i == 0 else jnp.where(masks[i], v, acc)
                both[h].append(acc)
                if h:
                    dst_ref[pl.ds(pl.multiple_of(g * 16, 16), 16), n * 128 : n * 128 + 128] = jnp.concatenate(
                        [both[0][n], acc], 0
                    ).astype(jnp.bfloat16)
        return 0

    lax.fori_loop(0, groups, body, 0)


def normed(h, gain):
    return h * lax.rsqrt(jnp.mean(h * h, axis=-1, keepdims=True) + EPS) * gain


def conv_kernel(
    second,
    idx_ref,
    plan_ref,
    counts_ref,
    lo_ref,
    mid_ref,
    hi_ref,
    w_in,
    gain_ref,
    *rest,
):
    if second:
        x_ref, wd_ref, gain_down_ref, place_ref, out_ref, down_ref, edge_ref, table, gathered, acc_ref, w_ref, self_ref, fine_ref, raw, placed = rest
    else:
        out_ref, table, gathered, acc_ref, w_ref, self_ref = rest
    step = pl.program_id(0)
    masks = sublane_masks()
    sub16 = lax.broadcasted_iota(jnp.int32, (8, 128), 0)

    @pl.when(step == 0)
    def _():
        table[:PAD, :] = jnp.zeros((PAD, 128), jnp.float32)
        w_ref[: SELF * 128, :] = w_in[: SELF * 128, :]
        w_ref[SELF * 128 :, :] = w_in[(SELF + 1) * 128 :, :]
        table[pl.ds(PAD, 1024), :] = lo_ref[...].astype(jnp.float32)
        if second:
            table[pl.ds(PAD + 1024, 4096), :] = mid_ref[...].astype(jnp.float32)
        else:

            def masked(g, _):
                for i in range(8):
                    block = g * 16 + 2 * i
                    row = pl.multiple_of(block * 8, 16)
                    valid = jnp.concatenate([sub16 < counts_ref[block], sub16 < counts_ref[block + 1]], 0)
                    value = jnp.where(valid, mid_ref[pl.ds(row, 16), :].astype(jnp.float32), 0.0)
                    table[pl.ds(pl.multiple_of(row + (PAD + 1024), 8), 16), :] = value
                return 0

            lax.fori_loop(0, 32, masked, 0)
        table[pl.ds(PAD + 5120, 1024), :] = hi_ref[...].astype(jnp.float32)

    plan = step * PLAN
    total = plan_ref[plan + LISTED + 128]
    gather_listed(idx_ref, plan_ref, plan, (total + 15) // 16, table, gathered, masks)
    own = mid_ref[pl.ds(pl.multiple_of(step * 1024, 1024), 1024), :]
    self_ref[...] = jnp.dot(own, w_in[SELF * 128 : (SELF + 1) * 128, :], preferred_element_type=jnp.float32)
    acc_ref[:MOSTLY, :] = jnp.dot(gathered[:MOSTLY, :], w_ref[...], preferred_element_type=jnp.float32)

    @pl.when(total > MOSTLY)
    def _():
        acc_ref[MOSTLY:1024, :] = jnp.dot(gathered[MOSTLY:, :], w_ref[...], preferred_element_type=jnp.float32)

    def epilogue(tile, _):
        gain = gain_ref[...]
        for i in range(GROUPS):
            start = plan_ref.at[pl.ds(plan + LISTED + tile * GROUPS * 2 + 2 * i, 2)]
            h = jnp.concatenate([acc_ref[pl.ds(start[0], 8), :], acc_ref[pl.ds(start[1], 8), :]], 0)
            h = normed(h + self_ref[pl.ds(pl.multiple_of(tile * TILE + i * 16, 16), 16), :], gain)
            row = pl.multiple_of(step * 1024 + tile * TILE + i * 16, 16)
            if second:
                h = x_ref[pl.ds(row, 16), :].astype(jnp.float32) + h
            block = step * 128 + tile * GROUPS * 2 + 2 * i
            valid = jnp.concatenate([sub16 < counts_ref[block], sub16 < counts_ref[block + 1]], 0)
            value = jnp.where(valid, jnp.maximum(h, 0.0), 0.0).astype(jnp.bfloat16)
            out_ref[pl.ds(row, 16), :] = value
            if second:
                fine_ref[pl.ds(row, 16), :] = value.astype(jnp.float32)
        return 0

    lax.fori_loop(0, 8, epilogue, 0)

    if second:

        @pl.when(step == 3)
        def _():

            def down(c, _):
                total = jnp.zeros((64, 256), jnp.float32)
                for j in range(8):
                    child = fine_ref[pl.ds(c * 512 + j, 64, stride=8), :].astype(jnp.bfloat16)
                    total += jnp.dot(child, wd_ref[j * 128 : (j + 1) * 128, :], preferred_element_type=jnp.float32)
                value = jnp.maximum(normed(total, gain_down_ref[...]), 0.0)
                row = pl.multiple_of(c * 64, 64)
                raw[pl.ds(row, 64), :] = value[:, :128]
                raw[pl.ds(row + 512, 64), :] = value[:, 128:]
                return 0

            lax.fori_loop(0, 8, down, 0)
            for n, row in enumerate((0, 448)):
                for h in range(2):
                    edge_ref[n * 64 : n * 64 + 64, h * 128 : h * 128 + 128] = raw[
                        h * 512 + row : h * 512 + row + 64, :
                    ].astype(jnp.bfloat16)
            placed[...] = jnp.zeros_like(placed)

            def put(g, _):
                for i in range(16):
                    at = place_ref[g * 16 + i]
                    placed[pl.ds(at, 1), :] = raw[pl.ds(g * 16 + i, 1), :]
                    placed[pl.ds(at + 520, 1), :] = raw[pl.ds(g * 16 + i + 512, 1), :]
                return 0

            lax.fori_loop(0, 32, put, 0)
            down_ref[:, :128] = placed[:512, :].astype(jnp.bfloat16)
            down_ref[:, 128:] = placed[520:1032, :].astype(jnp.bfloat16)


def whole(shape):
    return pl.BlockSpec(shape, lambda i: (0,) * len(shape))


def conv(second, idx, plan, counts, lo, mid, hi, w, gain, *more, places=()):
    specs = [
        pl.BlockSpec((8 * K * TILE,), lambda i: (i,), memory_space=pltpu.SMEM),
        pl.BlockSpec(memory_space=pltpu.SMEM),
        pl.BlockSpec(memory_space=pltpu.SMEM),
    ] + [whole(a.shape) for a in (lo, mid, hi, w, gain) + more]
    specs += [pl.BlockSpec(memory_space=pltpu.SMEM) for _ in places]
    out_shape = [jax.ShapeDtypeStruct((4096, 128), jnp.bfloat16)]
    scratch = [
        pltpu.VMEM((PAD + 6144 + 8, 128), jnp.float32),
        pltpu.VMEM((1024, len(OTHERS) * 128), jnp.bfloat16),
        pltpu.VMEM((1024 + 8, 128), jnp.float32),
        pltpu.VMEM((len(OTHERS) * 128, 128), jnp.bfloat16),
        pltpu.VMEM((1024, 128), jnp.float32),
    ]
    if second:
        out_shape.append(jax.ShapeDtypeStruct((512, 256), jnp.bfloat16))
        out_shape.append(jax.ShapeDtypeStruct((128, 256), jnp.bfloat16))
        scratch.append(pltpu.VMEM((4096, 128), jnp.float32))
        scratch.append(pltpu.VMEM((1024, 128), jnp.float32))
        scratch.append(pltpu.VMEM((1040, 128), jnp.float32))
    return pl.pallas_call(
        functools.partial(conv_kernel, second),
        grid=(4,),
        in_specs=specs,
        out_specs=[whole(s.shape) for s in out_shape],
        out_shape=out_shape,
        scratch_shapes=scratch,
        name="conv_second" if second else "conv_first",
        compiler_params=pltpu.CompilerParams(vmem_limit_bytes=VMEM_LIMIT),
    )(idx, plan, counts, lo, mid, hi, w, gain, *more, *places)


HALF = 2048 + 16
NOWHERE = PAD + 2048
REACH = 640


def ring(axis):
    me, count = lax.axis_index(axis), lax.axis_size(axis)
    return lax.rem(me + 1, count), lax.rem(me + count - 1, count)


def greet(partners):
    barrier = pltpu.get_barrier_semaphore()
    for partner in partners:
        pl.semaphore_signal(barrier, inc=1, device_id=partner, device_id_type=pl.DeviceIdType.MESH)
    pl.semaphore_wait(barrier, len(partners))


def sender(send_sem, recv_sem):
    count = [0]

    def send(src, dst, partner):
        n = count[0]
        count[0] += 1
        copy = pltpu.make_async_remote_copy(
            src_ref=src,
            dst_ref=dst,
            send_sem=send_sem.at[n],
            recv_sem=recv_sem.at[n],
            device_id=partner,
            device_id_type=pl.DeviceIdType.MESH,
        )
        copy.start()
        return copy

    return send


def halo_kernel(field_ref, lo_ref, hi_ref, send_sem, recv_sem):
    tile = lax.axis_index("tile")
    above, below = ring("morton")
    greet([(tile, above), (tile, below)])
    send = sender(send_sem, recv_sem)
    copies = [
        send(field_ref.at[pl.ds(3072, 1024)], lo_ref, (tile, above)),
        send(field_ref.at[pl.ds(0, 1024)], hi_ref, (tile, below)),
    ]
    for copy in copies:
        copy.wait()


def halo_of(field):
    return pl.pallas_call(
        halo_kernel,
        in_specs=[pl.BlockSpec(memory_space=pl.ANY)],
        out_specs=[pl.BlockSpec(memory_space=pl.ANY)] * 2,
        out_shape=[jax.ShapeDtypeStruct((1024, 128), jnp.bfloat16)] * 2,
        scratch_shapes=[pltpu.SemaphoreType.DMA((2,)), pltpu.SemaphoreType.DMA((2,))],
        name="halo",
        compiler_params=pltpu.CompilerParams(collective_id=1, has_side_effects=True),
    )(field)


def exchange_kernel(rows_ref, edge_ref, codes_ref, pool_ref, places_ref, send_sem, recv_sem, local_sem):
    tile, me = lax.axis_index("tile"), lax.axis_index("morton")
    right, left = ring("tile")
    above, below = ring("morton")
    opposite = lax.rem(tile + 2, lax.axis_size("tile"))
    tiles = (tile, right, left, opposite)
    greet([(right, me), (left, me)] + [(t, m) for t in tiles for m in (above, below)])

    send = sender(send_sem, recv_sem)
    first, last = pl.ds(0, 256), pl.ds(256, 256)
    from_below, from_above = pl.ds(512, 64), pl.ds(576, 64)
    right_first = send(rows_ref.at[first], pool_ref.at[tile, first], (right, me))
    left_last = send(rows_ref.at[last], pool_ref.at[tile, last], (left, me))
    handed = {}
    for n, t in enumerate((right, left, tile)):
        handed[n, 0] = send(edge_ref.at[pl.ds(64, 64)], pool_ref.at[tile, from_below], (t, above))
        handed[n, 1] = send(edge_ref.at[pl.ds(0, 64)], pool_ref.at[tile, from_above], (t, below))
    others = [send(rows_ref.at[last], pool_ref.at[tile, last], (right, me))]
    others.append(send(rows_ref.at[first], pool_ref.at[tile, first], (left, me)))
    for t in tiles:
        others.append(send(codes_ref, places_ref.at[0, tile], (t, above)))
        others.append(send(codes_ref, places_ref.at[1, tile], (t, below)))
    own = pltpu.make_async_copy(rows_ref, pool_ref.at[tile, pl.ds(0, 512)], local_sem)
    own.start()

    relays = ((right_first, left, first, right), (left_last, right, last, left))
    relays += ((handed[0, 0], left, from_below, right), (handed[1, 1], right, from_above, left))
    passed = []
    for copy, source, part, target in relays:
        copy.wait_recv()
        passed.append(send(pool_ref.at[source, part], pool_ref.at[source, part], (target, me)))
    for copy, _, _, _ in relays:
        copy.wait_send()
    own.wait()
    for copy in [handed[0, 1], handed[1, 0], handed[2, 0], handed[2, 1]] + others + passed:
        copy.wait()


def exchange(rows, edges, codes):
    return pl.pallas_call(
        exchange_kernel,
        in_specs=[pl.BlockSpec(memory_space=pl.ANY)] * 3,
        out_specs=[pl.BlockSpec(memory_space=pl.ANY)] * 2,
        out_shape=[
            jax.ShapeDtypeStruct((4, REACH, 256), jnp.bfloat16),
            jax.ShapeDtypeStruct((2, 4, 1, 128), jnp.int32),
        ],
        scratch_shapes=[
            pltpu.SemaphoreType.DMA((22,)),
            pltpu.SemaphoreType.DMA((22,)),
            pltpu.SemaphoreType.DMA,
        ],
        name="exchange",
        compiler_params=pltpu.CompilerParams(collective_id=0, has_side_effects=True),
    )(rows, edges, codes)


def coarse_kernel(idx_ref, places_ref, pool_ref, w_in, gain_ref, out_ref, table, source, gathered, acc_ref):
    masks = sublane_masks()
    table[:PAD, :] = jnp.zeros((PAD, 128), jnp.float32)
    table[HALF : HALF + PAD, :] = jnp.zeros((PAD, 128), jnp.float32)

    def tile_rows(t, _):
        row = pl.multiple_of(PAD + t * 512, 8)
        for h in range(2):
            cols = slice(h * 128, h * 128 + 128)
            table[pl.ds(row + h * HALF, 512), :] = pool_ref[t, :512, cols].astype(jnp.float32)
            source[pl.ds((t * 2 + h) * 128, 128), :] = pool_ref[t, 512:, cols].astype(jnp.float32)
        return 0

    lax.fori_loop(0, 4, tile_rows, 0)

    def handed(t, _):
        for kind in range(2):
            for i in range(64):
                at = places_ref[kind, t, 0, kind * 64 + i]
                row = t * 256 + kind * 64 + i
                table[pl.ds(at, 1), :] = source[pl.ds(row, 1), :]
                table[pl.ds(at + HALF, 1), :] = source[pl.ds(row + 128, 1), :]
        return 0

    lax.fori_loop(0, 4, handed, 0)
    gather_rows(idx_ref, ((table, 0), (table, HALF)), gathered, 4, masks)
    acc_ref[...] = jnp.dot(gathered[...], w_in[...], preferred_element_type=jnp.float32)
    first = PAD + 512 * lax.axis_index("tile")

    def epilogue(tile, _):
        for i in range(GROUPS):
            row = pl.multiple_of(tile * TILE + i * 16, 16)
            h = normed(acc_ref[pl.ds(row, 16), :], gain_ref[...])
            at = pl.multiple_of(first + row, 8)
            own = jnp.concatenate([table[pl.ds(at, 16), :], table[pl.ds(at + HALF, 16), :]], 1)
            out_ref[pl.ds(row, 16), :] = jnp.maximum(own + h, 0.0).astype(jnp.bfloat16)
        return 0

    lax.fori_loop(0, 4, epilogue, 0)


def coarse(idx, places, pool, w, gain):
    return pl.pallas_call(
        coarse_kernel,
        in_specs=[pl.BlockSpec(memory_space=pltpu.SMEM)] * 2 + [pl.BlockSpec(memory_space=pltpu.VMEM)] * 3,
        out_specs=pl.BlockSpec(memory_space=pltpu.VMEM),
        out_shape=jax.ShapeDtypeStruct((512, 256), jnp.bfloat16),
        scratch_shapes=[
            pltpu.VMEM((2 * HALF, 128), jnp.float32),
            pltpu.VMEM((1024, 128), jnp.float32),
            pltpu.VMEM((512, K * 256), jnp.bfloat16),
            pltpu.VMEM((512, 256), jnp.float32),
        ],
        name="coarse",
        compiler_params=pltpu.CompilerParams(vmem_limit_bytes=VMEM_LIMIT),
    )(idx, places, pool, w, gain)


def by_tiles(index):
    return index.reshape(K, -1, 1, TILE).transpose(1, 0, 2, 3).reshape(-1)


def plan_of(counts):
    held = counts.reshape(4, 128)
    block = jnp.arange(128, dtype=jnp.int32)
    ends = jnp.sum(jnp.where(block[None, :] <= block[:, None], held[:, None, :], 0), axis=-1)
    place = jnp.arange(LISTED, dtype=jnp.int32)
    past = ends[:, None, :] <= place[None, :, None]
    at = jnp.sum(past.astype(jnp.int32), axis=-1)
    start = jnp.max(jnp.where(past, ends[:, None, :], 0), axis=-1)
    entry = (at // 16) * (K * TILE) + (at % 16) * 8 + place[None, :] - start
    listed = jnp.where(at < 128, entry, 0)
    rest = jnp.broadcast_to(ends[:, 127:], (4, PLAN - LISTED - 128))
    return jnp.concatenate([listed, ends - held, rest], axis=1).reshape(-1)


def shards(
    features,
    neighbours,
    counts,
    owner,
    slot,
    coarse_neighbours,
    w_first,
    w_second,
    w_down,
    w_coarse,
    gain_first,
    gain_second,
    gain_down,
    gain_coarse,
):
    lane_ids = jnp.arange(8, dtype=jnp.int32)

    def masked(first):
        valid = lane_ids[None, :] < counts[0, first : first + 128, None]
        rows = features[0, 8 * first : 8 * first + 1024].reshape(128, 8, 128)
        return jnp.where(valid[:, :, None], rows, 0).astype(jnp.bfloat16).reshape(1024, 128)

    lo, hi = shifted(masked(384), "morton", 1), shifted(masked(0), "morton", -1)
    by_offset = neighbours[0].T
    local = by_offset + jnp.arange(4096, dtype=jnp.int32)[None, :]
    idx = by_tiles(jnp.where(by_offset < 0, -1, local))
    plan = plan_of(counts[0])
    coarse_idx = by_tiles(coarse_neighbours[0].T)

    me = lax.axis_index("morton")
    destination = owner[0]
    at = PAD + 512 * lax.axis_index("tile") + slot[0]

    def handed(to):
        return jnp.where(destination == to, at, NOWHERE)

    edges = jnp.concatenate([handed(me + 1)[448:], handed(me - 1)[:64]])
    codes = edges[None]
    kept = jnp.where(destination == me, slot[0], 512)

    (act,) = conv(False, idx, plan, counts[0], lo, features[0], hi, w_first, gain_first[None])
    lo, hi = halo_of(act)
    fine, rows, edge_rows = conv(
        True, idx, plan, counts[0], lo, act, hi, w_second, gain_second[None], features[0], w_down, gain_down[None], places=(kept,)
    )
    pool, places = exchange(rows, edge_rows, codes)
    out = coarse(coarse_idx, places, pool, w_coarse, gain_coarse[None])
    return fine[None], out[None]


def solution(mesh):
    split = P("tile", "morton", None)
    flat = P("tile", "morton")
    in_specs = (split, split, flat, flat, flat, split) + (P(),) * 8
    return jax.shard_map(shards, mesh=mesh, in_specs=in_specs, out_specs=(split, split), check_vma=False)
```
